256 devices in a mesh: seq: 16 (over y, x_hi, core), tp: 16 (over x_lo, z).
Axes of the slice: x: 4 (x_hi: 2, x_lo: 2; x = x_hi * 2 + x_lo), y: 4, z: 8, core: 2. Of those that a mesh axis runs over, the one named last changes fastest.
Arguments:
- tokens: bfloat16 [8192, 4096], P('seq', 'tp'), may hold values from -24 to 24
- query_weight: bfloat16 [4096, 4096], P(None, 'tp'), may hold values from -0.09375 to 0.09375
- kv_weight: bfloat16 [2, 4096, 1024], P(None, 'seq'), may hold values from -0.09375 to 0.09375
- out_weight: bfloat16 [4096, 4096], P('tp'), may hold values from -0.75 to 0.75
Outputs:
- attended: bfloat16 [8192, 4096], P('seq', 'tp')
The draws below stay inside these ranges and needn't reach their ends.
All inputs are finite; a program needn't handle non-finite values.
Results may differ from the reference program's by a relative error of at most 0.024.
Values may be sent and summed in bfloat16 or wider, within the bound.
No kernel may reach another device: no remote copies, remote signals or barrier semaphores. Data moves between devices by JAX's collectives and lax.ppermute only.
A program may use at most 64 MiB of HBM per device.

```python
import jax
import jax.numpy as jnp
from jax import lax

D = 4096
HEADS = 32
KV_HEADS = 8
HD = 128
TOKENS = 8192
N_TP = 16


def draw_tokens(key, part):
    key = jax.random.fold_in(key, 7)
    base = jax.random.normal(jax.random.fold_in(key, 1), (TOKENS, D), jnp.float32)
    return jnp.clip(base, -24.0, 24.0).astype(jnp.bfloat16)


def level_of(own_key, dims, split, low, top_value):
    loudness = 1.0
    for axis_at, blocks in split:
        heights = jax.random.uniform(jax.random.fold_in(jax.random.fold_in(own_key, 6), axis_at), (blocks,), jnp.float32, low / len(split), top_value / len(split))
        loudness = loudness * jnp.repeat(jnp.exp(heights), dims[axis_at] // blocks).reshape((-1,) + (1,) * (len(dims) - 1 - axis_at))
    return loudness


def normal_values(rng, extent, width, most, shards=(), kind=jnp.bfloat16):
    drawn = jax.random.normal(rng, extent, jnp.float32) * width
    if len(shards) > 0:
        drawn = level_of(rng, extent, shards, -0.22, 0.18) * drawn
    return jnp.clip(drawn, min=-most, max=most).astype(kind)


def setup_inputs(seed: int = 0) -> dict:
    streams_of = jax.random.split(jax.random.key(seed), 5)
    return {
        "tokens": draw_tokens(jax.random.fold_in(streams_of[4], 71), 0),
        "query_weight": normal_values(streams_of[1], (D, HEADS * HD), D ** -0.5, 0.09375, ((1, 16),)),
        "kv_weight": normal_values(streams_of[2], (2, D, KV_HEADS * HD), D ** -0.5, 0.09375, ((1, 16),)),
        "out_weight": normal_values(streams_of[3], (HEADS * HD, D), (HD // 2) ** -0.5, 0.75, ((0, 16),)),
    }


rotary_base = 500000.0
masked_score = -1e30


def rotate(vectors, positions):
    half_size = vectors.shape[-1] // 2
    frequency = rotary_base ** (-jnp.arange(half_size, dtype=jnp.float32) / half_size)
    angles = positions.astype(jnp.float32)[:, None] * frequency[None, :]
    cosine = jnp.cos(angles)[:, None, :]
    sine_part = jnp.sin(angles)[:, None, :]
    first_half = vectors[..., :half_size]
    second_half = vectors[..., half_size:]
    return jnp.concatenate([first_half * cosine - second_half * sine_part, second_half * cosine + first_half * sine_part], -1)


def reference(tokens, query_weight, kv_weight, out_weight):
    length = tokens.shape[0]
    positions = jnp.arange(length, dtype=jnp.int32)
    queries = jnp.dot(tokens, query_weight, preferred_element_type=jnp.float32).reshape(length, HEADS, HD)
    queries = rotate(queries, positions).astype(jnp.bfloat16)
    key_block = jnp.dot(tokens, kv_weight[0], preferred_element_type=jnp.float32).reshape(length, KV_HEADS, HD)
    key_block = rotate(key_block, positions).astype(jnp.bfloat16)
    value_block = jnp.dot(tokens, kv_weight[1], preferred_element_type=jnp.float32).astype(jnp.bfloat16)
    value_block = value_block.reshape(length, KV_HEADS, HD)
    score_scale = HD ** -0.5
    visible = positions[None, :] <= positions[:, None]
    group_size = HEADS // KV_HEADS
    query_heads = jnp.transpose(queries, (1, 0, 2))
    key_heads = jnp.transpose(key_block, (1, 0, 2))
    value_heads = jnp.transpose(value_block, (1, 0, 2))
    head_ids = jnp.arange(HEADS, dtype=jnp.int32)

    def one_head(inputs):
        query_head, head_id = inputs
        kv_id = (head_id // group_size).astype(jnp.int32)
        key_head = lax.dynamic_index_in_dim(key_heads, kv_id, 0, keepdims=False)
        value_head = lax.dynamic_index_in_dim(value_heads, kv_id, 0, keepdims=False)
        scores = jnp.dot(query_head, key_head.T, preferred_element_type=jnp.float32) * score_scale
        scores = jnp.where(visible, scores, masked_score)
        row_max = jnp.max(scores, -1, keepdims=True)
        weights = jnp.where(visible, jnp.exp(scores - row_max), 0.0)
        row_total = jnp.sum(weights, -1, keepdims=True)
        context = jnp.dot(weights.astype(jnp.bfloat16), value_head, preferred_element_type=jnp.float32) / row_total
        return context.astype(jnp.bfloat16)

    contexts = lax.map(one_head, (query_heads, head_ids))
    contexts = jnp.transpose(contexts, (1, 0, 2)).reshape(length, HEADS * HD)
    group_rows = HEADS * HD // N_TP
    summed = jnp.zeros((length, out_weight.shape[1]), jnp.float32)
    for group in range(N_TP):
        piece = jnp.dot(contexts[:, group * group_rows:(group + 1) * group_rows],
                        out_weight[group * group_rows:(group + 1) * group_rows],
                        preferred_element_type=jnp.float32).astype(jnp.bfloat16)
        piece = lax.optimization_barrier(piece)
        summed = summed + piece.astype(jnp.float32)
    return summed.astype(jnp.bfloat16)
```

```python
import functools

import jax
import jax.numpy as jnp
from jax import lax
from jax.experimental import pallas as pl
from jax.experimental.pallas import tpu as pltpu
from jax.sharding import PartitionSpec as P

HEADS = 32
KV_HEADS = 8
HD = 128
ROTARY_BASE = 500000.0
MASKED = -1e30
BOTH = ("seq", "tp")
NY, NH, NC, NL, NZ = 4, 2, 2, 2, 8
NX = NH * NL
BLOCK = 256


def linear(y, h, c, l, z):
    return ((y * NH + h) * NC + c) * (NL * NZ) + l * NZ + z


def routes(move):
    pairs = []
    for y in range(NY):
        for h in range(NH):
            for c in range(NC):
                for l in range(NL):
                    for z in range(NZ):
                        pairs.append((linear(y, h, c, l, z), linear(*move(y, h, c, l, z))))
    return pairs


def swap_route(shift):
    return routes(lambda y, h, c, l, z: (y, h, l, c, (z + shift) % NZ))


def z_route(shift):
    return routes(lambda y, h, c, l, z: (y, h, c, l, (z + shift) % NZ))


def y_route(shift):
    return routes(lambda y, h, c, l, z: ((y + shift) % NY, h, c, l, z))


def x_route(shift):
    def move(y, h, c, l, z):
        x = (h * NL + l + shift) % NX
        return y, x // NL, c, x % NL, z

    return routes(move)


CORE_ROUTE = routes(lambda y, h, c, l, z: (y, h, 1 - c, l, z))
PAIR_ROUTE = routes(lambda y, h, c, l, z: (y, h, c, 1 - l, z))
FLIP_ROUTE = routes(lambda y, h, c, l, z: (y, 1 - h, c, 1 - l, z))


def send(value, route):
    return lax.ppermute(value, BOTH, route)


def project_kernel(rows, place, *refs):
    blocks = refs[: 2 * NZ]
    wq, wkv, cosine, sine, q_out, k_out, v_out = refs[2 * NZ :]
    y, h, c, z = place[0], place[1], place[2], place[4]
    acc_q = jnp.zeros((rows, 2 * HD), jnp.float32)
    acc_kv = jnp.zeros((rows, 2 * HD), jnp.float32)
    for i in range(NZ):
        for j in range(2):
            core = c if j == 0 else 1 - c
            feature = core * NZ + lax.rem(z + i, NZ)
            block = blocks[2 * i + j][...]
            acc_q += jnp.dot(
                block,
                wq[pl.ds(pl.multiple_of(feature * BLOCK, BLOCK), BLOCK), :],
                preferred_element_type=jnp.float32,
            )
            fy = feature // 4
            fh = lax.rem(feature // 2, 2)
            fc = lax.rem(feature, 2)
            at = (lax.rem(fy - y + NY, NY) * 2 + lax.rem(fh + h, 2)) * 2 + lax.rem(fc + c, 2)
            acc_kv += jnp.dot(block, wkv[at], preferred_element_type=jnp.float32)
    cos = cosine[...]
    sin = sine[...]

    def rotate(vectors):
        half = HD // 2
        turned = jnp.concatenate([vectors[:, half:], vectors[:, :half]], 1)
        return vectors * cos + turned * sin

    scale = HD**-0.5 * 1.4426950408889634
    q_out[:rows] = (rotate(acc_q[:, :HD]) * scale).astype(jnp.bfloat16)
    q_out[rows:] = (rotate(acc_q[:, HD:]) * scale).astype(jnp.bfloat16)
    k_out[...] = rotate(acc_kv[:, :HD]).astype(jnp.bfloat16)
    v_out[...] = acc_kv[:, HD:].astype(jnp.bfloat16)


def project(place, blocks, wq, wkv, cosine, sine):
    rows = blocks[0].shape[0]
    vmem = pl.BlockSpec(memory_space=pltpu.VMEM)
    out = jax.ShapeDtypeStruct((rows, HD), jnp.bfloat16)
    return pl.pallas_call(
        functools.partial(project_kernel, rows),
        out_shape=(jax.ShapeDtypeStruct((2 * rows, HD), jnp.bfloat16), out, out),
        in_specs=[pl.BlockSpec(memory_space=pltpu.SMEM)] + [vmem] * (len(blocks) + 4),
        out_specs=(vmem, vmem, vmem),
        compiler_params=pltpu.CompilerParams(vmem_limit_bytes=48 * 2**20),
        cost_estimate=pl.CostEstimate(
            flops=2 * rows * 4096 * 512, bytes_accessed=8 * 2**20, transcendentals=0
        ),
    )(place, *blocks, wq, wkv, cosine, sine)


def attend_kernel(rows, place, q_ref, *refs):
    k_parts, v_parts = refs[:5], refs[5:10]
    out, keys, values, top, total, acc, sems = refs[10:]
    y, x = place[0], place[5]
    copies = []

    def start(source, target):
        copy = pltpu.make_async_copy(source, target, sems.at[len(copies)])
        copy.start()
        copies.append(copy)

    start(k_parts[0], keys.at[0:4])
    start(v_parts[0], values.at[0:4])
    start(k_parts[1], keys.at[4:8])
    start(k_parts[2], keys.at[8:10])
    start(k_parts[3], keys.at[10:12])
    start(k_parts[4], keys.at[12:16])
    start(v_parts[1], values.at[4:8])
    start(v_parts[2], values.at[8:10])
    start(v_parts[3], values.at[10:12])
    start(v_parts[4], values.at[12:16])

    def scores_of(key_block):
        return lax.dot_general(
            q_ref[...], key_block, (((1,), (1,)), ((), ())), preferred_element_type=jnp.float32
        )

    def wide(column):
        return jnp.concatenate([column] * (rows // HD), 1)

    copies[0].wait()
    copies[1].wait()
    scores = scores_of(keys[0])
    query_at = lax.rem(lax.broadcasted_iota(jnp.int32, scores.shape, 0), rows)
    key_at = lax.broadcasted_iota(jnp.int32, scores.shape, 1)
    scores = jnp.where(key_at <= query_at, scores, MASKED)
    peak = jnp.broadcast_to(jnp.max(scores, axis=1, keepdims=True), (2 * rows, HD))
    weights = jnp.exp2(scores - wide(peak))
    top[...] = peak
    total[...] = jnp.broadcast_to(jnp.sum(weights, axis=1, keepdims=True), (2 * rows, HD))
    acc[...] = jnp.dot(
        weights.astype(jnp.bfloat16), values[0], preferred_element_type=jnp.float32
    )
    for copy in copies[2:]:
        copy.wait()
    mine = y * NX + x

    def step(block, carry):
        dy, dx = block // 4, lax.rem(block, 4)
        theirs = lax.rem(y + dy, NY) * NX + lax.rem(x + dx, NX)
        value_at = dx * 4 + dy

        @pl.when(theirs < mine)
        def _():
            scores = scores_of(keys[block])
            old = top[...]
            peak = jnp.maximum(old, jnp.max(scores, axis=1, keepdims=True))
            weights = jnp.exp2(scores - wide(peak))
            factor = jnp.exp2(old - peak)
            total[...] = total[...] * factor + jnp.sum(weights, axis=1, keepdims=True)
            acc[...] = acc[...] * factor + jnp.dot(
                weights.astype(jnp.bfloat16), values[value_at], preferred_element_type=jnp.float32
            )
            top[...] = peak

        return carry

    lax.fori_loop(1, NX * NY, step, 0)
    context = acc[...] / total[...]
    out[...] = jnp.concatenate([context[:rows], context[rows:]], 1).astype(jnp.bfloat16)


def attend(place, queries, k_parts, v_parts):
    rows = queries.shape[0] // 2
    vmem = pl.BlockSpec(memory_space=pltpu.VMEM)
    anywhere = pl.BlockSpec(memory_space=pl.ANY)
    held = pltpu.VMEM((NX * NY, rows, HD), jnp.bfloat16)
    wide = pltpu.VMEM((2 * rows, HD), jnp.float32)
    return pl.pallas_call(
        functools.partial(attend_kernel, rows),
        out_shape=jax.ShapeDtypeStruct((rows, 2 * HD), jnp.bfloat16),
        in_specs=[pl.BlockSpec(memory_space=pltpu.SMEM), vmem] + [anywhere] * 10,
        out_specs=vmem,
        scratch_shapes=[held, held, wide, wide, wide, pltpu.SemaphoreType.DMA((10,))],
        compiler_params=pltpu.CompilerParams(vmem_limit_bytes=48 * 2**20),
        cost_estimate=pl.CostEstimate(
            flops=4 * 2 * rows * 8192 * HD, bytes_accessed=4 * 2**20, transcendentals=16 * rows * rows
        ),
    )(place, queries, *k_parts, *v_parts)


def gather_features(tokens):
    half = tokens.shape[0] // 2
    own = [None] * NZ
    own[0] = send(tokens, swap_route(0))
    own[7] = send(tokens, swap_route(1))
    own[1] = send(tokens, swap_route(-1))
    own[6] = send(own[7], z_route(1))
    own[2] = send(own[1], z_route(-1))
    own[5] = send(own[6], z_route(1))
    own[3] = send(own[2], z_route(-1))
    first = send(own[5][:half], z_route(1))
    second = send(own[3][half:], z_route(-1))
    own[4] = jnp.concatenate([first, second], 0)
    blocks = []
    for block in own:
        blocks += [block, send(block, CORE_ROUTE)]
    return blocks


def gather_kv_weight(kv_weight, c, z):
    def columns(core):
        part = lax.dynamic_slice_in_dim(kv_weight, (core * 4 + z // 2) * HD, HD, 2)
        return jnp.concatenate([part[0], part[1]], 1)

    pair = jnp.stack([columns(c), send(columns(1 - c), CORE_ROUTE)])
    four = jnp.stack([pair, send(pair, FLIP_ROUTE)])
    after = send(four, y_route(-1))
    before = send(four, y_route(1))
    far = jnp.stack([send(after[0], y_route(-1)), send(before[1], y_route(1))])
    return jnp.stack([four, after, far, before]).reshape(16, BLOCK, 2 * HD)


def gather_rows(block, first, second):
    half = block.shape[0] // 2
    after = send(block, first(-1))
    before = send(block, first(1))
    far = jnp.concatenate([send(after[:half], first(-1)), send(before[half:], first(1))], 0)
    line = jnp.stack([block, after, far, before])
    after = send(line, second(-1))
    before = send(line, second(1))
    far_low = send(after[:2], second(-1))
    far_high = send(before[2:], second(1))
    return [line, after, far_low, far_high, before]


def scatter_sums(part_of):
    def rounded(value):
        return value.astype(jnp.bfloat16)

    far = part_of(4)
    half = far.shape[0] // 2
    up = send(rounded(far[:half]), z_route(1))
    down = send(rounded(far[half:]), z_route(-1))
    here = part_of(3)
    up = rounded(here + jnp.pad(up, ((0, half), (0, 0))).astype(jnp.float32))
    here = part_of(5)
    down = rounded(here + jnp.pad(down, ((half, 0), (0, 0))).astype(jnp.float32))
    up = send(up, z_route(1))
    down = send(down, z_route(-1))
    up = send(rounded(part_of(2) + up.astype(jnp.float32)), z_route(1))
    down = send(rounded(part_of(6) + down.astype(jnp.float32)), z_route(-1))
    up = send(rounded(part_of(1) + up.astype(jnp.float32)), swap_route(1))
    down = send(rounded(part_of(7) + down.astype(jnp.float32)), swap_route(-1))
    middle = send(rounded(part_of(0)), swap_route(0))
    return rounded(
        up.astype(jnp.float32) + down.astype(jnp.float32) + middle.astype(jnp.float32)
    )


def shards(tokens, query_weight, kv_weight, out_weight):
    rows = tokens.shape[0]
    seq_rank = lax.axis_index("seq")
    tp_rank = lax.axis_index("tp")
    y, h, c = seq_rank // 4, (seq_rank // 2) % 2, seq_rank % 2
    l, z = tp_rank // NZ, tp_rank % NZ
    x = h * NL + l
    place = jnp.stack([y, h, c, l, z, x]).astype(jnp.int32)

    blocks = gather_features(tokens)
    wq = send(query_weight, swap_route(0))
    wkv = gather_kv_weight(kv_weight, c, z)

    positions = ((y * NX + x) * rows + jnp.arange(rows, dtype=jnp.int32)).astype(jnp.float32)
    frequency = ROTARY_BASE ** (-jnp.arange(HD // 2, dtype=jnp.float32) / (HD // 2))
    angles = positions[:, None] * frequency[None, :]
    cosine, sine = jnp.cos(angles), jnp.sin(angles)
    cosine = jnp.concatenate([cosine, cosine], 1)
    sine = jnp.concatenate([-sine, sine], 1)

    queries, keys, values = project(place, blocks, wq, wkv, cosine, sine)
    k_parts = gather_rows(keys, x_route, y_route)
    v_parts = gather_rows(values, y_route, x_route)

    half_columns = out_weight.shape[1] // 2
    own = lax.dynamic_slice_in_dim(out_weight, c * half_columns, half_columns, 1)
    other = send(own, PAIR_ROUTE)
    wo = jnp.concatenate([jnp.where(l == c, own, other), jnp.where(l == c, other, own)], 0)

    context = attend(place, queries, k_parts, v_parts)
    context = jnp.concatenate([context, send(context, CORE_ROUTE)], 1)

    def part_of(distance):
        at = ((z + distance) % NZ) * BLOCK
        columns = lax.dynamic_slice_in_dim(wo, at, BLOCK, 1)
        return jnp.dot(context, columns, preferred_element_type=jnp.float32)

    return scatter_sums(part_of)


def solution(mesh):
    return jax.shard_map(
        shards,
        mesh=mesh,
        in_specs=(P("seq", "tp"), P(None, "tp"), P(None, "seq", None), P("tp", None)),
        out_specs=P("seq", "tp"),
        check_vma=False,
    )
```

```python
import functools

import jax
import jax.numpy as jnp
from jax import lax
from jax.experimental import pallas as pl
from jax.experimental.pallas import tpu as pltpu
from jax.sharding import PartitionSpec as P

HEADS = 32
KV_HEADS = 8
HD = 128
ROTARY_BASE = 500000.0
MASKED = -1e30
BOTH = ("seq", "tp")
NY, NH, NC, NL, NZ = 4, 2, 2, 2, 8
NX = NH * NL
BLOCK = 256
ARRIVAL = (0, 7, 1, 6, 2, 5, 3, 4)


def linear(y, h, c, l, z):
    return ((y * NH + h) * NC + c) * (NL * NZ) + l * NZ + z


def routes(move):
    pairs = []
    for y in range(NY):
        for h in range(NH):
            for c in range(NC):
                for l in range(NL):
                    for z in range(NZ):
                        pairs.append((linear(y, h, c, l, z), linear(*move(y, h, c, l, z))))
    return pairs


def swap_route(shift):
    return routes(lambda y, h, c, l, z: (y, h, l, c, (z + shift) % NZ))


def z_route(shift):
    return routes(lambda y, h, c, l, z: (y, h, c, l, (z + shift) % NZ))


def y_route(shift):
    return routes(lambda y, h, c, l, z: ((y + shift) % NY, h, c, l, z))


def x_route(shift):
    def move(y, h, c, l, z):
        x = (h * NL + l + shift) % NX
        return y, x // NL, c, x % NL, z

    return routes(move)


def line_route(shift):
    over_x, over_y = x_route(shift), y_route(shift)
    return routes_by_core(over_x, over_y)


def cross_route(shift):
    over_x, over_y = x_route(shift), y_route(shift)
    return routes_by_core(over_y, over_x)


def routes_by_core(first, second):
    pairs = []
    for one, other in zip(first, second):
        core = one[0] // (NL * NZ) % NC
        pairs.append(one if core == 0 else other)
    return pairs


CORE_ROUTE = routes(lambda y, h, c, l, z: (y, h, 1 - c, l, z))
PAIR_ROUTE = routes(lambda y, h, c, l, z: (y, h, c, 1 - l, z))
FLIP_ROUTE = routes(lambda y, h, c, l, z: (y, 1 - h, c, 1 - l, z))
FLIP_CORE_ROUTE = routes(lambda y, h, c, l, z: (y, 1 - h, 1 - c, 1 - l, z))
Z_BY_CORE = routes_by_core(z_route(1), z_route(-1))


def send(value, route):
    return lax.ppermute(value, BOTH, route)


SWAP = [(source, target) for source, target in swap_route(0) if source != target]


def send_swapped(value, same):
    return jnp.where(same, value, send(value, SWAP))


def rotated(vectors, cos, sin):
    half = HD // 2
    turned = jnp.concatenate([vectors[:, half:], vectors[:, :half]], 1)
    return vectors * cos + turned * sin


def project_rows(place, blocks, weight_of):
    c, z = place[2], place[4]
    acc = None
    for distance in ARRIVAL:
        for j in range(2):
            core = c if j == 0 else 1 - c
            feature = core * NZ + lax.rem(z + distance, NZ)
            part = jnp.dot(
                blocks[2 * distance + j][...],
                weight_of(feature),
                preferred_element_type=jnp.float32,
            )
            acc = part if acc is None else acc + part
    return acc


def project_kv_kernel(place, *refs):
    blocks, parts = refs[: 2 * NZ], refs[2 * NZ : 2 * NZ + 5]
    cosine, sine, out, wkv = refs[2 * NZ + 5 :]
    y, h, c = place[0], place[1], place[2]
    at = 0
    for part in parts:
        count = part.shape[0]
        wkv[at : at + count] = part[...]
        at += count

    def weight_of(feature):
        dy = lax.rem(feature // 4 - y + NY, NY)
        dh = lax.rem(lax.rem(feature // 2, 2) + h, 2)
        dc = lax.rem(lax.rem(feature, 2) + c, 2)
        return wkv[(dy * 2 + dh) * 2 + dc]

    acc = project_rows(place, blocks, weight_of)
    out[:, :HD] = rotated(acc[:, :HD], cosine[...], sine[...]).astype(jnp.bfloat16)
    out[:, HD:] = acc[:, HD:].astype(jnp.bfloat16)


def project_q_kernel(rows, place, *refs):
    blocks = refs[: 2 * NZ]
    own_wq, moved_wq = refs[2 * NZ : 2 * NZ + 2]
    cosine, sine, out, wq, sem = refs[2 * NZ + 2 :]
    c, l = place[2], place[3]
    fetch_own = pltpu.make_async_copy(own_wq, wq, sem)
    fetch_moved = pltpu.make_async_copy(moved_wq, wq, sem)

    @pl.when(c == l)
    def _():
        fetch_own.start()

    @pl.when(c != l)
    def _():
        fetch_moved.start()

    fetch_own.wait()

    def weight_of(feature):
        return wq[pl.ds(pl.multiple_of(feature * BLOCK, BLOCK), BLOCK), :]

    acc = project_rows(place, blocks, weight_of)
    scale = HD**-0.5 * 1.4426950408889634
    for head in range(2):
        turned = rotated(acc[:, head * HD : (head + 1) * HD], cosine[...], sine[...])
        out[head * rows : (head + 1) * rows] = (turned * scale).astype(jnp.bfloat16)


VMEM = pl.BlockSpec(memory_space=pltpu.VMEM)
SMEM = pl.BlockSpec(memory_space=pltpu.SMEM)
ANYWHERE = pl.BlockSpec(memory_space=pl.ANY)
PARAMS = pltpu.CompilerParams(vmem_limit_bytes=48 * 2**20)


def project_kv(place, blocks, parts, cosine, sine):
    rows = blocks[0].shape[0]
    return pl.pallas_call(
        project_kv_kernel,
        out_shape=jax.ShapeDtypeStruct((rows, 2 * HD), jnp.bfloat16),
        in_specs=[SMEM] + [VMEM] * (len(blocks) + len(parts) + 2),
        out_specs=VMEM,
        scratch_shapes=[pltpu.VMEM((16, BLOCK, 2 * HD), jnp.bfloat16)],
        compiler_params=PARAMS,
        cost_estimate=pl.CostEstimate(
            flops=2 * rows * 4096 * 2 * HD, bytes_accessed=6 * 2**20, transcendentals=0
        ),
    )(place, *blocks, *parts, cosine, sine)


def project_q(place, blocks, own_wq, moved_wq, cosine, sine):
    rows = blocks[0].shape[0]
    return pl.pallas_call(
        functools.partial(project_q_kernel, rows),
        out_shape=jax.ShapeDtypeStruct((2 * rows, HD), jnp.bfloat16),
        in_specs=[SMEM] + [VMEM] * len(blocks) + [ANYWHERE] * 2 + [VMEM] * 2,
        out_specs=VMEM,
        scratch_shapes=[pltpu.VMEM(own_wq.shape, jnp.bfloat16), pltpu.SemaphoreType.DMA],
        compiler_params=PARAMS,
        cost_estimate=pl.CostEstimate(
            flops=2 * rows * 4096 * 2 * HD, bytes_accessed=6 * 2**20, transcendentals=0
        ),
    )(place, *blocks, own_wq, moved_wq, cosine, sine)


def attend_kernel(rows, steps, first, last, place, query, *refs):
    lines = refs[: len(steps)]
    refs = refs[len(steps) :]
    if not first:
        old_state, refs = refs[:3], refs[3:]
    if last:
        out, top, total, acc = refs
    else:
        top, total, acc = refs
    y, c, x = place[0], place[2], place[5]
    mine = y * NX + x

    def merge(held, block, begin):
        keys = held[block, :, :HD]
        values = held[block, :, HD:]
        scores = lax.dot_general(
            query[...], keys, (((1,), (1,)), ((), ())), preferred_element_type=jnp.float32
        )
        if begin:
            query_at = lax.rem(lax.broadcasted_iota(jnp.int32, scores.shape, 0), rows)
            key_at = lax.broadcasted_iota(jnp.int32, scores.shape, 1)
            scores = jnp.where(key_at <= query_at, scores, MASKED)
            peak = jnp.max(scores, axis=1, keepdims=True)
            peak = jnp.broadcast_to(peak, (2 * rows, HD))
        else:
            old = top[...]
            peak = jnp.maximum(old, jnp.max(scores, axis=1, keepdims=True))
        weights = jnp.exp2(scores - jnp.concatenate([peak] * (rows // HD), 1))
        sums = jnp.sum(weights, axis=1, keepdims=True)
        part = jnp.dot(weights.astype(jnp.bfloat16), values, preferred_element_type=jnp.float32)
        if begin:
            total[...] = jnp.broadcast_to(sums, (2 * rows, HD))
            acc[...] = part
        else:
            factor = jnp.exp2(old - peak)
            total[...] = total[...] * factor + sums
            acc[...] = acc[...] * factor + part
        top[...] = peak

    if not first:
        for new, old in zip((top, total, acc), old_state):
            new[...] = old[...]
    if first:
        merge(lines[0], 0, True)
    for line, (outer, begin, count) in zip(lines, steps):

        def step(block, carry, line=line, outer=outer, begin=begin):
            inner = block + begin
            dy = jnp.where(c == 0, outer, inner)
            dx = jnp.where(c == 0, inner, outer)
            theirs = lax.rem(y + dy, NY) * NX + lax.rem(x + dx, NX)

            @pl.when(theirs < mine)
            def _():
                merge(line, block, False)

            return carry

        lax.fori_loop(1 if first else 0, count, step, 0)
    if last:
        context = acc[...] / total[...]
        out[...] = jnp.concatenate([context[:rows], context[rows:]], 1).astype(jnp.bfloat16)


def attend(place, query, lines, steps, state, last):
    rows = query.shape[0] // 2
    count = sum(count for _, _, count in steps)
    wide = (2 * rows, HD)
    scratch = []
    if last:
        out_shape = jax.ShapeDtypeStruct((rows, 2 * HD), jnp.bfloat16)
        out_specs = VMEM
        scratch += [pltpu.VMEM(wide, jnp.float32)] * 3
    else:
        out_shape = (jax.ShapeDtypeStruct(wide, jnp.float32),) * 3
        out_specs = (VMEM,) * 3
    return pl.pallas_call(
        functools.partial(attend_kernel, rows, steps, not state, last),
        out_shape=out_shape,
        in_specs=[SMEM, VMEM] + [VMEM] * (len(lines) + len(state)),
        out_specs=out_specs,
        scratch_shapes=scratch,
        compiler_params=PARAMS,
        cost_estimate=pl.CostEstimate(
            flops=4 * 2 * rows * count * rows * HD,
            bytes_accessed=count * rows * 4 * HD,
            transcendentals=2 * rows * count * rows,
        ),
    )(place, query, *lines, *state)


def gather_inputs(tokens, query_weight, kv_weight, c, z, same):
    def columns(core):
        part = lax.dynamic_slice_in_dim(kv_weight, (core * 4 + z // 2) * HD, HD, 2)
        return jnp.concatenate([part[0], part[1]], 1)

    mine, other = columns(c), columns(1 - c)
    own = [None] * NZ
    own[7] = send(tokens, swap_route(1))
    own[1] = send(tokens, swap_route(-1))
    own[0] = send_swapped(tokens, same)
    pieces = [
        mine,
        send(other, CORE_ROUTE),
        send(mine, FLIP_ROUTE),
        send(other, FLIP_CORE_ROUTE),
    ]
    own[0], own[1], own[7], pieces, query_weight = lax.optimization_barrier(
        (own[0], own[1], own[7], pieces, query_weight)
    )
    four = jnp.stack(pieces)
    after = send(four, y_route(-1))
    before = send(four, y_route(1))
    moved_wq = send(query_weight, SWAP)
    own[6] = send(own[7], z_route(1))
    own[2] = send(own[1], z_route(-1))
    own[5] = send(own[6], z_route(1))
    own[3] = send(own[2], z_route(-1))
    own[5], own[3], after, before = lax.optimization_barrier((own[5], own[3], after, before))
    far_low = send(after[:2], y_route(-1))
    far_high = send(before[2:], y_route(1))
    own[4] = send(jnp.where(c == 0, own[5], own[3]), Z_BY_CORE)
    blocks = []
    for block in own:
        blocks += [block, send(block, CORE_ROUTE)]
    return blocks, [four, after, far_low, far_high, before], query_weight, moved_wq


def scatter_sums(part_of, c, same):
    def rounded(value):
        return value.astype(jnp.bfloat16)

    far = send(rounded(part_of(4)), Z_BY_CORE).astype(jnp.float32)
    up = send(rounded(part_of(3) + jnp.where(c == 0, far, 0.0)), z_route(1))
    down = send(rounded(part_of(5) + jnp.where(c == 0, 0.0, far)), z_route(-1))
    middle = send_swapped(rounded(part_of(0)), same)
    up = send(rounded(part_of(2) + up.astype(jnp.float32)), z_route(1))
    down = send(rounded(part_of(6) + down.astype(jnp.float32)), z_route(-1))
    up = send(rounded(part_of(1) + up.astype(jnp.float32)), swap_route(1))
    down = send(rounded(part_of(7) + down.astype(jnp.float32)), swap_route(-1))
    return rounded(
        up.astype(jnp.float32) + down.astype(jnp.float32) + middle.astype(jnp.float32)
    )


def shards(tokens, query_weight, kv_weight, out_weight):
    rows = tokens.shape[0]
    seq_rank = lax.axis_index("seq")
    tp_rank = lax.axis_index("tp")
    y, h, c = seq_rank // 4, (seq_rank // 2) % 2, seq_rank % 2
    l, z = tp_rank // NZ, tp_rank % NZ
    x = h * NL + l
    place = jnp.stack([y, h, c, l, z, x]).astype(jnp.int32)
    same = c == l

    blocks, wkv_parts, query_weight, moved_wq = gather_inputs(
        tokens, query_weight, kv_weight, c, z, same
    )

    positions = ((y * NX + x) * rows + jnp.arange(rows, dtype=jnp.int32)).astype(jnp.float32)
    frequency = ROTARY_BASE ** (-jnp.arange(HD // 2, dtype=jnp.float32) / (HD // 2))
    angles = positions[:, None] * frequency[None, :]
    cosine, sine = jnp.cos(angles), jnp.sin(angles)
    cosine = jnp.concatenate([cosine, cosine], 1)
    sine = jnp.concatenate([-sine, sine], 1)

    half_columns = out_weight.shape[1] // 2
    wo = lax.dynamic_slice_in_dim(out_weight, c * half_columns, half_columns, 1)
    wo = jnp.concatenate([wo, wo], 1)
    wo = lax.dynamic_slice_in_dim(wo, ((z + 2) % NZ) * BLOCK, half_columns, 1)
    near, last = wo[:, : half_columns // 2], wo[:, half_columns // 2 :]

    block = project_kv(place, blocks, wkv_parts, cosine, sine)
    line = jnp.stack(
        [
            block,
            send(block, line_route(-1)),
            send(block, line_route(2)),
            send(block, line_route(1)),
        ]
    )
    query = project_q(place, blocks, query_weight, moved_wq, cosine, sine)
    line, query = lax.optimization_barrier((line, query))
    after = send(line, cross_route(-1))
    before = send(line, cross_route(1))
    state = attend(place, query, [line], ((0, 0, 4),), (), False)
    after, before, state = lax.optimization_barrier((after, before, state))
    far_low = send(after[:2], cross_route(-1))
    far_high = send(before[2:], cross_route(1))

    near, _ = lax.optimization_barrier((near, moved_wq))
    near = jnp.concatenate([near, send(near, PAIR_ROUTE)], 0)
    last, far_low = lax.optimization_barrier((last, far_low))
    last = jnp.concatenate([last, send(last, PAIR_ROUTE)], 0)

    state = attend(place, query, [after, before], ((1, 0, 4), (3, 0, 4)), state, False)
    context = attend(
        place, query, [far_low, far_high], ((2, 0, 2), (2, 2, 2)), state, True
    )
    other = send(context, CORE_ROUTE)
    context = jnp.concatenate(
        [jnp.where(same, context, other), jnp.where(same, other, context)], 1
    )

    def part_of(distance):
        at = (distance - 2) % NZ
        piece = near if at < 4 else last
        at = (at % 4) * BLOCK
        return jnp.dot(context, piece[:, at : at + BLOCK], preferred_element_type=jnp.float32)

    return scatter_sums(part_of, c, same)


def solution(mesh):
    return jax.shard_map(
        shards,
        mesh=mesh,
        in_specs=(P("seq", "tp"), P(None, "tp"), P(None, "seq", None), P("tp", None)),
        out_specs=P("seq", "tp"),
        check_vma=False,
    )
```

```python
import functools

import jax
import jax.numpy as jnp
from jax import lax
from jax.experimental import pallas as pl
from jax.experimental.pallas import tpu as pltpu
from jax.sharding import PartitionSpec as P

HEADS = 32
KV_HEADS = 8
HD = 128
ROTARY_BASE = 500000.0
MASKED = -1e30
BOTH = ("seq", "tp")
NY, NH, NC, NL, NZ = 4, 2, 2, 2, 8
NX = NH * NL
BLOCK = 256
ARRIVAL = (0, 1, 7, 2, 6, 3, 5, 4)


def linear(y, h, c, l, z):
    return ((y * NH + h) * NC + c) * (NL * NZ) + l * NZ + z


def routes(move):
    pairs = []
    for y in range(NY):
        for h in range(NH):
            for c in range(NC):
                for l in range(NL):
                    for z in range(NZ):
                        pairs.append((linear(y, h, c, l, z), linear(*move(y, h, c, l, z))))
    return pairs


def sign_of(core):
    return 1 if core == 0 else -1


def swap_route(shift):
    return routes(lambda y, h, c, l, z: (y, h, l, c, (z + sign_of(l) * shift) % NZ))


def swap_back_route(shift):
    return routes(lambda y, h, c, l, z: (y, h, l, c, (z + shift) % NZ))


def z_chain(shift):
    return routes(lambda y, h, c, l, z: (y, h, c, l, (z + sign_of(c) * shift) % NZ))


def y_chain(shift):
    return routes(lambda y, h, c, l, z: ((y + sign_of(c) * shift) % NY, h, c, l, z))


def z_route(shift):
    return routes(lambda y, h, c, l, z: (y, h, c, l, (z + shift) % NZ))


def y_route(shift):
    return routes(lambda y, h, c, l, z: ((y + shift) % NY, h, c, l, z))


def x_route(shift):
    def move(y, h, c, l, z):
        x = (h * NL + l + shift) % NX
        return y, x // NL, c, x % NL, z

    return routes(move)


def line_route(shift):
    over_x, over_y = x_route(shift), y_route(shift)
    return routes_by_core(over_x, over_y)


def cross_route(shift):
    over_x, over_y = x_route(shift), y_route(shift)
    return routes_by_core(over_y, over_x)


def routes_by_core(first, second):
    pairs = []
    for one, other in zip(first, second):
        core = one[0] // (NL * NZ) % NC
        pairs.append(one if core == 0 else other)
    return pairs


CORE_ROUTE = routes(lambda y, h, c, l, z: (y, h, 1 - c, l, z))
PAIR_ROUTE = routes(lambda y, h, c, l, z: (y, h, c, 1 - l, z))
FLIP_ROUTE = routes(lambda y, h, c, l, z: (y, 1 - h, c, 1 - l, z))
FLIP_CORE_ROUTE = routes(lambda y, h, c, l, z: (y, 1 - h, 1 - c, 1 - l, z))
Z_BY_CORE = routes_by_core(z_route(1), z_route(-1))


def send(value, route):
    return lax.ppermute(value, BOTH, route)


SWAP = [(source, target) for source, target in swap_route(0) if source != target]


def send_swapped(value, same):
    return jnp.where(same, value, send(value, SWAP))


def rotated(vectors, cos, sin):
    half = HD // 2
    turned = jnp.concatenate([vectors[:, half:], vectors[:, :half]], 1)
    return vectors * cos + turned * sin


def project_rows(place, blocks, weight_of):
    c, z = place[2], place[4]
    acc = None
    for steps in ARRIVAL:
        for j in range(2):
            core = c if j == 0 else 1 - c
            feature = core * NZ + lax.rem(z + (2 * core - 1) * steps + NZ, NZ)
            part = jnp.dot(
                blocks[2 * steps + j][...],
                weight_of(feature),
                preferred_element_type=jnp.float32,
            )
            acc = part if acc is None else acc + part
    return acc


def project_kv_kernel(place, *refs):
    blocks, parts = refs[: 2 * NZ], refs[2 * NZ : 2 * NZ + 4]
    cosine, sine, out, wkv = refs[2 * NZ + 4 :]
    y, h, c = place[0], place[1], place[2]
    at = 0
    for part in parts:
        count = part.shape[0]
        wkv[at : at + count] = part[...]
        at += count

    def weight_of(feature):
        dy = lax.rem((2 * c - 1) * (feature // 4 - y) + NY, NY)
        dh = lax.rem(lax.rem(feature // 2, 2) + h, 2)
        dc = lax.rem(lax.rem(feature, 2) + c, 2)
        return wkv[(dy * 2 + dh) * 2 + dc]

    acc = project_rows(place, blocks, weight_of)
    out[:, :HD] = rotated(acc[:, :HD], cosine[...], sine[...]).astype(jnp.bfloat16)
    out[:, HD:] = acc[:, HD:].astype(jnp.bfloat16)


def project_q_kernel(rows, place, *refs):
    blocks = refs[: 2 * NZ]
    own_wq, moved_wq = refs[2 * NZ : 2 * NZ + 2]
    cosine, sine, out, wq, sem = refs[2 * NZ + 2 :]
    c, l = place[2], place[3]
    fetch_own = pltpu.make_async_copy(own_wq, wq, sem)
    fetch_moved = pltpu.make_async_copy(moved_wq, wq, sem)

    @pl.when(c == l)
    def _():
        fetch_own.start()

    @pl.when(c != l)
    def _():
        fetch_moved.start()

    fetch_own.wait()

    def weight_of(feature):
        return wq[pl.ds(pl.multiple_of(feature * BLOCK, BLOCK), BLOCK), :]

    acc = project_rows(place, blocks, weight_of)
    scale = HD**-0.5 * 1.4426950408889634
    for head in range(2):
        turned = rotated(acc[:, head * HD : (head + 1) * HD], cosine[...], sine[...])
        out[head * rows : (head + 1) * rows] = (turned * scale).astype(jnp.bfloat16)


VMEM = pl.BlockSpec(memory_space=pltpu.VMEM)
SMEM = pl.BlockSpec(memory_space=pltpu.SMEM)
ANYWHERE = pl.BlockSpec(memory_space=pl.ANY)
PARAMS = pltpu.CompilerParams(vmem_limit_bytes=48 * 2**20)


def project_kv(place, blocks, parts, cosine, sine):
    rows = blocks[0].shape[0]
    return pl.pallas_call(
        project_kv_kernel,
        out_shape=jax.ShapeDtypeStruct((rows, 2 * HD), jnp.bfloat16),
        in_specs=[SMEM] + [VMEM] * (len(blocks) + len(parts) + 2),
        out_specs=VMEM,
        scratch_shapes=[pltpu.VMEM((16, BLOCK, 2 * HD), jnp.bfloat16)],
        compiler_params=PARAMS,
        cost_estimate=pl.CostEstimate(
            flops=2 * rows * 4096 * 2 * HD, bytes_accessed=6 * 2**20, transcendentals=0
        ),
    )(place, *blocks, *parts, cosine, sine)


def project_q(place, blocks, own_wq, moved_wq, cosine, sine):
    rows = blocks[0].shape[0]
    return pl.pallas_call(
        functools.partial(project_q_kernel, rows),
        out_shape=jax.ShapeDtypeStruct((2 * rows, HD), jnp.bfloat16),
        in_specs=[SMEM] + [VMEM] * len(blocks) + [ANYWHERE] * 2 + [VMEM] * 2,
        out_specs=VMEM,
        scratch_shapes=[pltpu.VMEM(own_wq.shape, jnp.bfloat16), pltpu.SemaphoreType.DMA],
        compiler_params=PARAMS,
        cost_estimate=pl.CostEstimate(
            flops=2 * rows * 4096 * 2 * HD, bytes_accessed=6 * 2**20, transcendentals=0
        ),
    )(place, *blocks, own_wq, moved_wq, cosine, sine)


def attend_kernel(rows, steps, first, last, place, query, *refs):
    lines = refs[: len(steps)]
    refs = refs[len(steps) :]
    if not first:
        old_state, refs = refs[:3], refs[3:]
    if last:
        out, top, total, acc = refs
    else:
        top, total, acc = refs
    y, c, x = place[0], place[2], place[5]
    mine = y * NX + x

    def merge(held, block, begin):
        keys = held[block, :, :HD]
        values = held[block, :, HD:]
        scores = lax.dot_general(
            query[...], keys, (((1,), (1,)), ((), ())), preferred_element_type=jnp.float32
        )
        if begin:
            query_at = lax.rem(lax.broadcasted_iota(jnp.int32, scores.shape, 0), rows)
            key_at = lax.broadcasted_iota(jnp.int32, scores.shape, 1)
            scores = jnp.where(key_at <= query_at, scores, MASKED)
            peak = jnp.max(scores, axis=1, keepdims=True)
            peak = jnp.broadcast_to(peak, (2 * rows, HD))
        else:
            old = top[...]
            peak = jnp.maximum(old, jnp.max(scores, axis=1, keepdims=True))
        weights = jnp.exp2(scores - jnp.concatenate([peak] * (rows // HD), 1))
        sums = jnp.sum(weights, axis=1, keepdims=True)
        part = jnp.dot(weights.astype(jnp.bfloat16), values, preferred_element_type=jnp.float32)
        if begin:
            total[...] = jnp.broadcast_to(sums, (2 * rows, HD))
            acc[...] = part
        else:
            factor = jnp.exp2(old - peak)
            total[...] = total[...] * factor + sums
            acc[...] = acc[...] * factor + part
        top[...] = peak

    if not first:
        for new, old in zip((top, total, acc), old_state):
            new[...] = old[...]
    if first:
        merge(lines[0], 0, True)
    for line, outer in zip(lines, steps):

        def step(block, carry, line=line, outer=outer):
            inner = lax.rem(4 - block, 4)
            dy = jnp.where(c == 0, outer, inner)
            dx = jnp.where(c == 0, inner, outer)
            theirs = lax.rem(y + dy, NY) * NX + lax.rem(x + dx, NX)

            @pl.when(theirs < mine)
            def _():
                merge(line, block, False)

            return carry

        lax.fori_loop(1 if first else 0, 4, step, 0)
    if last:
        context = acc[...] / total[...]
        out[...] = jnp.concatenate([context[:rows], context[rows:]], 1).astype(jnp.bfloat16)


def attend(place, query, lines, steps, state, last):
    rows = query.shape[0] // 2
    count = 4 * len(steps)
    wide = (2 * rows, HD)
    scratch = []
    if last:
        out_shape = jax.ShapeDtypeStruct((rows, 2 * HD), jnp.bfloat16)
        out_specs = VMEM
        scratch += [pltpu.VMEM(wide, jnp.float32)] * 3
    else:
        out_shape = (jax.ShapeDtypeStruct(wide, jnp.float32),) * 3
        out_specs = (VMEM,) * 3
    return pl.pallas_call(
        functools.partial(attend_kernel, rows, steps, not state, last),
        out_shape=out_shape,
        in_specs=[SMEM, VMEM] + [VMEM] * (len(lines) + len(state)),
        out_specs=out_specs,
        scratch_shapes=scratch,
        compiler_params=PARAMS,
        cost_estimate=pl.CostEstimate(
            flops=4 * 2 * rows * count * rows * HD,
            bytes_accessed=count * rows * 4 * HD,
            transcendentals=2 * rows * count * rows,
        ),
    )(place, query, *lines, *state)


def gather_inputs(tokens, query_weight, kv_weight, out_weight, c, z, same):
    def columns(core):
        part = lax.dynamic_slice_in_dim(kv_weight, (core * 4 + z // 2) * HD, HD, 2)
        return jnp.concatenate([part[0], part[1]], 1)

    mine, other = columns(c), columns(1 - c)
    own = [None] * NZ
    own[1] = send(tokens, swap_route(1))
    own[7] = send(tokens, swap_route(-1))
    own[0] = send_swapped(tokens, same)
    flipped = send(jnp.stack([mine, other]), FLIP_ROUTE)
    own[0], own[1], own[7], flipped, query_weight, out_weight = lax.optimization_barrier(
        (own[0], own[1], own[7], flipped, query_weight, out_weight)
    )
    others = send(jnp.stack([other, flipped[1]]), CORE_ROUTE)
    four = jnp.stack([mine, others[0], flipped[0], others[1]])
    first = send(four, y_chain(1))
    second = send(four, y_chain(-1))
    moved_wq = send(query_weight, SWAP)
    own[2] = send(own[1], z_chain(1))
    own[6] = send(own[7], z_chain(-1))
    own[3] = send(own[2], z_chain(1))
    own[5] = send(own[6], z_chain(-1))
    own[3], own[5], first, second = lax.optimization_barrier((own[3], own[5], first, second))
    far = send(first, y_chain(1))
    own[4] = send(own[3], z_chain(1))
    blocks = []
    for block in own:
        blocks += [block, send(block, CORE_ROUTE)]
    half_columns = out_weight.shape[1] // 2
    wo = lax.dynamic_slice_in_dim(out_weight, c * half_columns, half_columns, 1)
    wo = jnp.concatenate([wo, wo], 1)
    wo = lax.dynamic_slice_in_dim(wo, ((z + 2) % NZ) * BLOCK, half_columns, 1)
    near, last = wo[:, : 5 * BLOCK], wo[:, 5 * BLOCK :]
    moved_near = send(near, PAIR_ROUTE)
    far, moved_wq, last = lax.optimization_barrier((far, moved_wq, last))
    return blocks, [four, first, far, second], query_weight, moved_wq, near, moved_near, last


def scatter_sums(part_of, c, same):
    def rounded(value):
        return value.astype(jnp.bfloat16)

    far = send(rounded(part_of(4)), Z_BY_CORE).astype(jnp.float32)
    up = send(rounded(part_of(3) + jnp.where(c == 0, far, 0.0)), z_route(1))
    down = send(rounded(part_of(5) + jnp.where(c == 0, 0.0, far)), z_route(-1))
    middle = send_swapped(rounded(part_of(0)), same)
    up = send(rounded(part_of(2) + up.astype(jnp.float32)), z_route(1))
    down = send(rounded(part_of(6) + down.astype(jnp.float32)), z_route(-1))
    up = send(rounded(part_of(1) + up.astype(jnp.float32)), swap_back_route(1))
    down = send(rounded(part_of(7) + down.astype(jnp.float32)), swap_back_route(-1))
    return rounded(
        up.astype(jnp.float32) + down.astype(jnp.float32) + middle.astype(jnp.float32)
    )


def shards(tokens, query_weight, kv_weight, out_weight):
    rows = tokens.shape[0]
    seq_rank = lax.axis_index("seq")
    tp_rank = lax.axis_index("tp")
    y, h, c = seq_rank // 4, (seq_rank // 2) % 2, seq_rank % 2
    l, z = tp_rank // NZ, tp_rank % NZ
    x = h * NL + l
    place = jnp.stack([y, h, c, l, z, x]).astype(jnp.int32)
    same = c == l

    blocks, wkv_parts, query_weight, moved_wq, near, moved_near, last = gather_inputs(
        tokens, query_weight, kv_weight, out_weight, c, z, same
    )

    positions = ((y * NX + x) * rows + jnp.arange(rows, dtype=jnp.int32)).astype(jnp.float32)
    frequency = ROTARY_BASE ** (-jnp.arange(HD // 2, dtype=jnp.float32) / (HD // 2))
    angles = positions[:, None] * frequency[None, :]
    cosine, sine = jnp.cos(angles), jnp.sin(angles)
    cosine = jnp.concatenate([cosine, cosine], 1)
    sine = jnp.concatenate([-sine, sine], 1)

    block = project_kv(place, blocks, wkv_parts, cosine, sine)
    line_first = send(block, line_route(1))
    line_second = send(block, line_route(-1))
    line_first, moved_near = lax.optimization_barrier((line_first, moved_near))
    line_far = send(line_first, line_route(1))
    query = project_q(place, blocks, query_weight, moved_wq, cosine, sine)
    line_far, line_second, query = lax.optimization_barrier((line_far, line_second, query))
    line = jnp.stack([block, line_first, line_far, line_second])
    first = send(line, cross_route(1))
    second = send(line, cross_route(-1))
    state = attend(place, query, [line], (0,), (), False)
    first, second, state = lax.optimization_barrier((first, second, state))
    far = send(first, cross_route(1))

    state = attend(place, query, [first, second], (3, 1), state, False)
    context = attend(place, query, [far], (2,), state, True)
    last, near, moved_near, context = lax.optimization_barrier((last, near, moved_near, context))
    near = jnp.concatenate([near, moved_near], 0)
    last = jnp.concatenate([last, send(last, PAIR_ROUTE)], 0)
    other = send(context, CORE_ROUTE)
    context = jnp.concatenate(
        [jnp.where(same, context, other), jnp.where(same, other, context)], 1
    )

    def part_of(distance):
        at = (distance - 2) % NZ
        piece, at = (near, at * BLOCK) if at < 5 else (last, (at - 5) * BLOCK)
        return jnp.dot(context, piece[:, at : at + BLOCK], preferred_element_type=jnp.float32)

    return scatter_sums(part_of, c, same)


def solution(mesh):
    return jax.shard_map(
        shards,
        mesh=mesh,
        in_specs=(P("seq", "tp"), P(None, "tp"), P(None, "seq", None), P("tp", None)),
        out_specs=P("seq", "tp"),
        check_vma=False,
    )
```

```python
import functools

import jax
import jax.numpy as jnp
from jax import lax
from jax.experimental import pallas as pl
from jax.experimental.pallas import tpu as pltpu
from jax.sharding import PartitionSpec as P

HEADS = 32
KV_HEADS = 8
HD = 128
ROTARY_BASE = 500000.0
MASKED = -1e30
BOTH = ("seq", "tp")
NY, NH, NC, NL, NZ = 4, 2, 2, 2, 8
NX = NH * NL
BLOCK = 256
ARRIVAL = (0, 1, 7, 2, 6, 3, 5, 4)
ORDER = (4, 5, 3, 6, 0, 2, 7, 1)


def linear(y, h, c, l, z):
    return ((y * NH + h) * NC + c) * (NL * NZ) + l * NZ + z


def routes(move):
    pairs = []
    for y in range(NY):
        for h in range(NH):
            for c in range(NC):
                for l in range(NL):
                    for z in range(NZ):
                        pairs.append((linear(y, h, c, l, z), linear(*move(y, h, c, l, z))))
    return pairs


def sign_of(core):
    return 1 if core == 0 else -1


def swap_route(shift):
    return routes(lambda y, h, c, l, z: (y, h, l, c, (z + sign_of(l) * shift) % NZ))


def swap_back_route(shift):
    return routes(lambda y, h, c, l, z: (y, h, l, c, (z + sign_of(c) * shift) % NZ))


def z_chain(shift):
    return routes(lambda y, h, c, l, z: (y, h, c, l, (z + sign_of(c) * shift) % NZ))


def y_chain(shift):
    return routes(lambda y, h, c, l, z: ((y + sign_of(c) * shift) % NY, h, c, l, z))


def z_route(shift):
    return routes(lambda y, h, c, l, z: (y, h, c, l, (z + shift) % NZ))


def y_route(shift):
    return routes(lambda y, h, c, l, z: ((y + shift) % NY, h, c, l, z))


def x_route(shift):
    def move(y, h, c, l, z):
        x = (h * NL + l + shift) % NX
        return y, x // NL, c, x % NL, z

    return routes(move)


def line_route(shift):
    over_x, over_y = x_route(shift), y_route(shift)
    return routes_by_core(over_x, over_y)


def cross_route(shift):
    over_x, over_y = x_route(shift), y_route(shift)
    return routes_by_core(over_y, over_x)


def routes_by_core(first, second):
    pairs = []
    for one, other in zip(first, second):
        core = one[0] // (NL * NZ) % NC
        pairs.append(one if core == 0 else other)
    return pairs


CORE_ROUTE = routes(lambda y, h, c, l, z: (y, h, 1 - c, l, z))
PAIR_ROUTE = routes(lambda y, h, c, l, z: (y, h, c, 1 - l, z))
FLIP_ROUTE = routes(lambda y, h, c, l, z: (y, 1 - h, c, 1 - l, z))


def send(value, route):
    return lax.ppermute(value, BOTH, route)


SWAP = [(source, target) for source, target in swap_route(0) if source != target]


def send_swapped(value, same):
    return jnp.where(same, value, send(value, SWAP))


def rotated(vectors, cos, sin):
    half = HD // 2
    turned = jnp.concatenate([vectors[:, half:], vectors[:, :half]], 1)
    return vectors * cos + turned * sin


def project_rows(place, blocks, weight_of):
    c, z = place[2], place[4]
    acc = None
    for steps in ARRIVAL:
        for j in range(2):
            core = c if j == 0 else 1 - c
            feature = core * NZ + lax.rem(z + (2 * core - 1) * steps + NZ, NZ)
            part = jnp.dot(
                blocks[2 * steps + j][...],
                weight_of(feature),
                preferred_element_type=jnp.float32,
            )
            acc = part if acc is None else acc + part
    return acc


def project_kv_kernel(place, *refs):
    blocks, parts = refs[: 2 * NZ], refs[2 * NZ : 2 * NZ + 4]
    cosine, sine, out, wkv = refs[2 * NZ + 4 :]
    y, h, c = place[0], place[1], place[2]
    at = 0
    for part in parts:
        count = part.shape[0]
        wkv[at : at + count] = part[...]
        at += count

    def weight_of(feature):
        dy = lax.rem((2 * c - 1) * (feature // 4 - y) + NY, NY)
        dh = lax.rem(lax.rem(feature // 2, 2) + h, 2)
        dc = lax.rem(lax.rem(feature, 2) + c, 2)
        return wkv[(dy * 2 + dh) * 2 + dc]

    acc = project_rows(place, blocks, weight_of)
    out[:, :HD] = rotated(acc[:, :HD], cosine[...], sine[...]).astype(jnp.bfloat16)
    out[:, HD:] = acc[:, HD:].astype(jnp.bfloat16)


def project_q_kernel(rows, place, *refs):
    blocks = refs[: 2 * NZ]
    own_wq, moved_wq = refs[2 * NZ : 2 * NZ + 2]
    cosine, sine, out, wq, sem = refs[2 * NZ + 2 :]
    c, l = place[2], place[3]
    fetch_own = pltpu.make_async_copy(own_wq, wq, sem)
    fetch_moved = pltpu.make_async_copy(moved_wq, wq, sem)

    @pl.when(c == l)
    def _():
        fetch_own.start()

    @pl.when(c != l)
    def _():
        fetch_moved.start()

    fetch_own.wait()

    def weight_of(feature):
        return wq[pl.ds(pl.multiple_of(feature * BLOCK, BLOCK), BLOCK), :]

    acc = project_rows(place, blocks, weight_of)
    scale = HD**-0.5 * 1.4426950408889634
    for head in range(2):
        turned = rotated(acc[:, head * HD : (head + 1) * HD], cosine[...], sine[...])
        out[head * rows : (head + 1) * rows] = (turned * scale).astype(jnp.bfloat16)


VMEM = pl.BlockSpec(memory_space=pltpu.VMEM)
SMEM = pl.BlockSpec(memory_space=pltpu.SMEM)
ANYWHERE = pl.BlockSpec(memory_space=pl.ANY)
PARAMS = pltpu.CompilerParams(vmem_limit_bytes=48 * 2**20)


def order_kernel(place, weight, near, last):
    c, z = place[2], place[4]
    for at, steps in enumerate(ORDER):
        column = c * NZ + lax.rem(z + (1 - 2 * c) * steps + NZ, NZ)
        piece = weight[:, pl.ds(pl.multiple_of(column * BLOCK, BLOCK), BLOCK)]
        if at < 5:
            near[:, at * BLOCK : (at + 1) * BLOCK] = piece
        else:
            last[:, (at - 5) * BLOCK : (at - 4) * BLOCK] = piece


def order_columns(place, weight):
    rows = weight.shape[0]
    return pl.pallas_call(
        order_kernel,
        out_shape=(
            jax.ShapeDtypeStruct((rows, 5 * BLOCK), weight.dtype),
            jax.ShapeDtypeStruct((rows, 3 * BLOCK), weight.dtype),
        ),
        in_specs=[SMEM, VMEM],
        out_specs=(VMEM, VMEM),
        compiler_params=PARAMS,
        cost_estimate=pl.CostEstimate(flops=0, bytes_accessed=2 * 2**20, transcendentals=0),
    )(place, weight)


def project_kv(place, blocks, parts, cosine, sine):
    rows = blocks[0].shape[0]
    return pl.pallas_call(
        project_kv_kernel,
        out_shape=jax.ShapeDtypeStruct((rows, 2 * HD), jnp.bfloat16),
        in_specs=[SMEM] + [VMEM] * (len(blocks) + len(parts) + 2),
        out_specs=VMEM,
        scratch_shapes=[pltpu.VMEM((16, BLOCK, 2 * HD), jnp.bfloat16)],
        compiler_params=PARAMS,
        cost_estimate=pl.CostEstimate(
            flops=2 * rows * 4096 * 2 * HD, bytes_accessed=6 * 2**20, transcendentals=0
        ),
    )(place, *blocks, *parts, cosine, sine)


def project_q(place, blocks, own_wq, moved_wq, cosine, sine):
    rows = blocks[0].shape[0]
    return pl.pallas_call(
        functools.partial(project_q_kernel, rows),
        out_shape=jax.ShapeDtypeStruct((2 * rows, HD), jnp.bfloat16),
        in_specs=[SMEM] + [VMEM] * len(blocks) + [ANYWHERE] * 2 + [VMEM] * 2,
        out_specs=VMEM,
        scratch_shapes=[pltpu.VMEM(own_wq.shape, jnp.bfloat16), pltpu.SemaphoreType.DMA],
        compiler_params=PARAMS,
        cost_estimate=pl.CostEstimate(
            flops=2 * rows * 4096 * 2 * HD, bytes_accessed=6 * 2**20, transcendentals=0
        ),
    )(place, *blocks, own_wq, moved_wq, cosine, sine)


def attend_kernel(rows, steps, first, last, place, query, *refs):
    lines = refs[: len(steps)]
    refs = refs[len(steps) :]
    if not first:
        old_state, refs = refs[:3], refs[3:]
    if last:
        out, top, total, acc = refs
    else:
        top, total, acc = refs
    y, c, x = place[0], place[2], place[5]
    mine = y * NX + x

    def merge(held, block, begin):
        keys = held[block, :, :HD]
        values = held[block, :, HD:]
        scores = lax.dot_general(
            query[...], keys, (((1,), (1,)), ((), ())), preferred_element_type=jnp.float32
        )
        if begin:
            query_at = lax.rem(lax.broadcasted_iota(jnp.int32, scores.shape, 0), rows)
            key_at = lax.broadcasted_iota(jnp.int32, scores.shape, 1)
            scores = jnp.where(key_at <= query_at, scores, MASKED)
            peak = jnp.max(scores, axis=1, keepdims=True)
            peak = jnp.broadcast_to(peak, (2 * rows, HD))
        else:
            old = top[...]
            peak = jnp.maximum(old, jnp.max(scores, axis=1, keepdims=True))
        weights = jnp.exp2(scores - jnp.concatenate([peak] * (rows // HD), 1))
        sums = jnp.sum(weights, axis=1, keepdims=True)
        part = jnp.dot(weights.astype(jnp.bfloat16), values, preferred_element_type=jnp.float32)
        if begin:
            total[...] = jnp.broadcast_to(sums, (2 * rows, HD))
            acc[...] = part
        else:
            factor = jnp.exp2(old - peak)
            total[...] = total[...] * factor + sums
            acc[...] = acc[...] * factor + part
        top[...] = peak

    if not first:
        for new, old in zip((top, total, acc), old_state):
            new[...] = old[...]
    if first:
        merge(lines[0], 0, True)
    for line, (outer, begin) in zip(lines, steps):

        def step(block, carry, line=line, outer=outer, begin=begin):
            inner = lax.rem(4 - begin - block, 4)
            dy = jnp.where(c == 0, outer, inner)
            dx = jnp.where(c == 0, inner, outer)
            theirs = lax.rem(y + dy, NY) * NX + lax.rem(x + dx, NX)

            @pl.when(theirs < mine)
            def _():
                merge(line, block, False)

            return carry

        lax.fori_loop(1 if first else 0, line.shape[0], step, 0)
    if last:
        context = acc[...] / total[...]
        out[...] = jnp.concatenate([context[:rows], context[rows:]], 1).astype(jnp.bfloat16)


def attend(place, query, lines, steps, state, last):
    rows = query.shape[0] // 2
    count = sum(line.shape[0] for line in lines)
    wide = (2 * rows, HD)
    scratch = []
    if last:
        out_shape = jax.ShapeDtypeStruct((rows, 2 * HD), jnp.bfloat16)
        out_specs = VMEM
        scratch += [pltpu.VMEM(wide, jnp.float32)] * 3
    else:
        out_shape = (jax.ShapeDtypeStruct(wide, jnp.float32),) * 3
        out_specs = (VMEM,) * 3
    return pl.pallas_call(
        functools.partial(attend_kernel, rows, steps, not state, last),
        out_shape=out_shape,
        in_specs=[SMEM, VMEM] + [VMEM] * (len(lines) + len(state)),
        out_specs=out_specs,
        scratch_shapes=scratch,
        compiler_params=PARAMS,
        cost_estimate=pl.CostEstimate(
            flops=4 * 2 * rows * count * rows * HD,
            bytes_accessed=count * rows * 4 * HD,
            transcendentals=2 * rows * count * rows,
        ),
    )(place, query, *lines, *state)


def gather_inputs(tokens, query_weight, kv_weight, out_weight, place, c, z, same):
    def columns(core):
        part = lax.dynamic_slice_in_dim(kv_weight, (core * 4 + z // 2) * HD, HD, 2)
        return jnp.concatenate([part[0], part[1]], 1)

    mine, other = columns(c), columns(1 - c)
    own = [None] * NZ
    own[1] = send(tokens, swap_route(1))
    own[7] = send(tokens, swap_route(-1))
    own[0] = send_swapped(tokens, same)
    flipped = send(jnp.stack([mine, other]), FLIP_ROUTE)
    own[0], own[1], own[7], flipped, query_weight, out_weight = lax.optimization_barrier(
        (own[0], own[1], own[7], flipped, query_weight, out_weight)
    )
    others = send(jnp.stack([other, flipped[1]]), CORE_ROUTE)
    four = jnp.stack([mine, others[0], flipped[0], others[1]])
    first = send(four, y_chain(1))
    second = send(four, y_chain(-1))
    moved_wq = send(query_weight, SWAP)
    own[2] = send(own[1], z_chain(1))
    own[6] = send(own[7], z_chain(-1))
    own[3] = send(own[2], z_chain(1))
    own[5] = send(own[6], z_chain(-1))
    own[3], own[5], first, second = lax.optimization_barrier((own[3], own[5], first, second))
    far = send(first, y_chain(1))
    own[4] = send(own[3], z_chain(1))
    blocks = []
    for block in own:
        blocks += [block, send(block, CORE_ROUTE)]
    near, last = order_columns(place, out_weight)
    moved_near = send(near, PAIR_ROUTE)
    far, moved_wq, last = lax.optimization_barrier((far, moved_wq, last))
    return blocks, [four, first, far, second], query_weight, moved_wq, near, moved_near, last


def scatter_sums(part_of, same):
    def add(part, arrived):
        return (part + arrived.astype(jnp.float32)).astype(jnp.bfloat16)

    long = send(part_of(4).astype(jnp.bfloat16), z_chain(1))
    short = send(part_of(5).astype(jnp.bfloat16), z_chain(-1))
    long = send(add(part_of(3), long), z_chain(1))
    short = send(add(part_of(6), short), z_chain(-1))
    middle = send_swapped(part_of(0).astype(jnp.bfloat16), same)
    long, short, middle = lax.optimization_barrier((long, short, middle))
    long = send(add(part_of(2), long), z_chain(1))
    short = send(add(part_of(7), short), swap_back_route(-1))
    long = send(add(part_of(1), long), swap_back_route(1))
    total = middle.astype(jnp.float32) + short.astype(jnp.float32) + long.astype(jnp.float32)
    return total.astype(jnp.bfloat16)


def shards(tokens, query_weight, kv_weight, out_weight):
    rows = tokens.shape[0]
    seq_rank = lax.axis_index("seq")
    tp_rank = lax.axis_index("tp")
    y, h, c = seq_rank // 4, (seq_rank // 2) % 2, seq_rank % 2
    l, z = tp_rank // NZ, tp_rank % NZ
    x = h * NL + l
    place = jnp.stack([y, h, c, l, z, x]).astype(jnp.int32)
    same = c == l

    blocks, wkv_parts, query_weight, moved_wq, near, moved_near, last = gather_inputs(
        tokens, query_weight, kv_weight, out_weight, place, c, z, same
    )

    positions = ((y * NX + x) * rows + jnp.arange(rows, dtype=jnp.int32)).astype(jnp.float32)
    frequency = ROTARY_BASE ** (-jnp.arange(HD // 2, dtype=jnp.float32) / (HD // 2))
    angles = positions[:, None] * frequency[None, :]
    cosine, sine = jnp.cos(angles), jnp.sin(angles)
    cosine = jnp.concatenate([cosine, cosine], 1)
    sine = jnp.concatenate([-sine, sine], 1)

    block = project_kv(place, blocks, wkv_parts, cosine, sine)
    line_first = send(block, line_route(1))
    line_second = send(block, line_route(-1))
    line_first, moved_near = lax.optimization_barrier((line_first, moved_near))
    line_far = send(line_first, line_route(1))
    query = project_q(place, blocks, query_weight, moved_wq, cosine, sine)
    line_far, line_second, query = lax.optimization_barrier((line_far, line_second, query))
    line = jnp.stack([block, line_first, line_far, line_second])
    first = send(line, cross_route(1))
    second = send(line, cross_route(-1))
    state = attend(place, query, [line], ((0, 0),), (), False)
    first, second, state = lax.optimization_barrier((first, second, state))
    far_low = send(first[:2], cross_route(1))
    far_high = send(second[2:], cross_route(-1))

    state = attend(place, query, [first, second], ((3, 0), (1, 0)), state, False)
    context = attend(place, query, [far_low, far_high], ((2, 0), (2, 2)), state, True)
    last, near, moved_near, context = lax.optimization_barrier((last, near, moved_near, context))
    near = jnp.concatenate([near, moved_near], 0)
    last = jnp.concatenate([last, send(last, PAIR_ROUTE)], 0)
    other = send(context, CORE_ROUTE)
    context = jnp.concatenate(
        [jnp.where(same, context, other), jnp.where(same, other, context)], 1
    )

    def part_of(steps):
        at = ORDER.index(steps)
        piece, at = (near, at * BLOCK) if at < 5 else (last, (at - 5) * BLOCK)
        return jnp.dot(context, piece[:, at : at + BLOCK], preferred_element_type=jnp.float32)

    return scatter_sums(part_of, same)


def solution(mesh):
    return jax.shard_map(
        shards,
        mesh=mesh,
        in_specs=(P("seq", "tp"), P(None, "tp"), P(None, "seq", None), P("tp", None)),
        out_specs=P("seq", "tp"),
        check_vma=False,
    )
```

```python
import functools

import jax
import jax.numpy as jnp
from jax import lax
from jax.experimental import pallas as pl
from jax.experimental.pallas import tpu as pltpu
from jax.sharding import PartitionSpec as P

HEADS = 32
KV_HEADS = 8
HD = 128
ROTARY_BASE = 500000.0
MASKED = -1e30
BOTH = ("seq", "tp")
NY, NH, NC, NL, NZ = 4, 2, 2, 2, 8
NX = NH * NL
BLOCK = 256
ARRIVAL = (0, 1, 7, 2, 6, 3, 5, 4)
ORDER = (4, 5, 3, 6, 0, 2, 7, 1)


def linear(y, h, c, l, z):
    return ((y * NH + h) * NC + c) * (NL * NZ) + l * NZ + z


def routes(move):
    pairs = []
    for y in range(NY):
        for h in range(NH):
            for c in range(NC):
                for l in range(NL):
                    for z in range(NZ):
                        pairs.append((linear(y, h, c, l, z), linear(*move(y, h, c, l, z))))
    return pairs


def sign_of(core):
    return 1 if core == 0 else -1


def swap_route(shift):
    return routes(lambda y, h, c, l, z: (y, h, l, c, (z + sign_of(l) * shift) % NZ))


def swap_back_route(shift):
    return routes(lambda y, h, c, l, z: (y, h, l, c, (z + sign_of(c) * shift) % NZ))


def z_chain(shift):
    return routes(lambda y, h, c, l, z: (y, h, c, l, (z + sign_of(c) * shift) % NZ))


def y_chain(shift):
    return routes(lambda y, h, c, l, z: ((y + sign_of(c) * shift) % NY, h, c, l, z))


def z_route(shift):
    return routes(lambda y, h, c, l, z: (y, h, c, l, (z + shift) % NZ))


def y_route(shift):
    return routes(lambda y, h, c, l, z: ((y + shift) % NY, h, c, l, z))


def x_route(shift):
    def move(y, h, c, l, z):
        x = (h * NL + l + shift) % NX
        return y, x // NL, c, x % NL, z

    return routes(move)


def line_route(shift):
    over_x, over_y = x_route(shift), y_route(shift)
    return routes_by_core(over_x, over_y)


def cross_route(shift):
    over_x, over_y = x_route(shift), y_route(shift)
    return routes_by_core(over_y, over_x)


def routes_by_core(first, second):
    pairs = []
    for one, other in zip(first, second):
        core = one[0] // (NL * NZ) % NC
        pairs.append(one if core == 0 else other)
    return pairs


CORE_ROUTE = routes(lambda y, h, c, l, z: (y, h, 1 - c, l, z))
PAIR_ROUTE = routes(lambda y, h, c, l, z: (y, h, c, 1 - l, z))
FLIP_ROUTE = routes(lambda y, h, c, l, z: (y, 1 - h, c, 1 - l, z))


def send(value, route):
    return lax.ppermute(value, BOTH, route)


SWAP = [(source, target) for source, target in swap_route(0) if source != target]


def send_swapped(value, same):
    return jnp.where(same, value, send(value, SWAP))


def rotated(vectors, cos, sin):
    half = HD // 2
    turned = jnp.concatenate([vectors[:, half:], vectors[:, :half]], 1)
    return vectors * cos + turned * sin


def project_rows(place, blocks, weight_of):
    c, z = place[2], place[4]
    acc = None
    for steps in ARRIVAL:
        for j in range(2):
            core = c if j == 0 else 1 - c
            feature = core * NZ + lax.rem(z + (2 * core - 1) * steps + NZ, NZ)
            part = jnp.dot(
                blocks[2 * steps + j][...],
                weight_of(feature),
                preferred_element_type=jnp.float32,
            )
            acc = part if acc is None else acc + part
    return acc


def project_kv_kernel(place, *refs):
    blocks, parts = refs[: 2 * NZ], refs[2 * NZ : 2 * NZ + 4]
    cosine, sine, out, wkv = refs[2 * NZ + 4 :]
    y, h, c = place[0], place[1], place[2]
    at = 0
    for part in parts:
        count = part.shape[0]
        wkv[at : at + count] = part[...]
        at += count

    def weight_of(feature):
        dy = lax.rem((2 * c - 1) * (feature // 4 - y) + NY, NY)
        dh = lax.rem(lax.rem(feature // 2, 2) + h, 2)
        dc = lax.rem(lax.rem(feature, 2) + c, 2)
        return wkv[(dy * 2 + dh) * 2 + dc]

    acc = project_rows(place, blocks, weight_of)
    out[:, :HD] = rotated(acc[:, :HD], cosine[...], sine[...]).astype(jnp.bfloat16)
    out[:, HD:] = acc[:, HD:].astype(jnp.bfloat16)


def project_q_kernel(rows, place, *refs):
    blocks = refs[: 2 * NZ]
    own_wq, moved_wq = refs[2 * NZ : 2 * NZ + 2]
    cosine, sine, out, wq, sem = refs[2 * NZ + 2 :]
    c, l = place[2], place[3]
    fetch_own = pltpu.make_async_copy(own_wq, wq, sem)
    fetch_moved = pltpu.make_async_copy(moved_wq, wq, sem)

    @pl.when(c == l)
    def _():
        fetch_own.start()

    @pl.when(c != l)
    def _():
        fetch_moved.start()

    fetch_own.wait()

    def weight_of(feature):
        return wq[pl.ds(pl.multiple_of(feature * BLOCK, BLOCK), BLOCK), :]

    acc = project_rows(place, blocks, weight_of)
    scale = HD**-0.5 * 1.4426950408889634
    for head in range(2):
        turned = rotated(acc[:, head * HD : (head + 1) * HD], cosine[...], sine[...])
        out[head * rows : (head + 1) * rows] = (turned * scale).astype(jnp.bfloat16)


VMEM = pl.BlockSpec(memory_space=pltpu.VMEM)
SMEM = pl.BlockSpec(memory_space=pltpu.SMEM)
ANYWHERE = pl.BlockSpec(memory_space=pl.ANY)
PARAMS = pltpu.CompilerParams(vmem_limit_bytes=48 * 2**20)


def order_kernel(place, weight, near, last):
    c, z = place[2], place[4]
    for at, steps in enumerate(ORDER):
        column = lax.rem(z + (1 - 2 * c) * steps + NZ, NZ)
        piece = weight[:, pl.ds(pl.multiple_of(column * BLOCK, BLOCK), BLOCK)]
        if at < 5:
            near[:, at * BLOCK : (at + 1) * BLOCK] = piece
        else:
            last[:, (at - 5) * BLOCK : (at - 4) * BLOCK] = piece


def order_columns(place, weight):
    rows = weight.shape[0]
    return pl.pallas_call(
        order_kernel,
        out_shape=(
            jax.ShapeDtypeStruct((rows, 5 * BLOCK), weight.dtype),
            jax.ShapeDtypeStruct((rows, 3 * BLOCK), weight.dtype),
        ),
        in_specs=[SMEM, VMEM],
        out_specs=(VMEM, VMEM),
        compiler_params=PARAMS,
        cost_estimate=pl.CostEstimate(flops=0, bytes_accessed=2 * 2**20, transcendentals=0),
    )(place, weight)


def project_kv(place, blocks, parts, cosine, sine):
    rows = blocks[0].shape[0]
    return pl.pallas_call(
        project_kv_kernel,
        out_shape=jax.ShapeDtypeStruct((rows, 2 * HD), jnp.bfloat16),
        in_specs=[SMEM] + [VMEM] * (len(blocks) + len(parts) + 2),
        out_specs=VMEM,
        scratch_shapes=[pltpu.VMEM((16, BLOCK, 2 * HD), jnp.bfloat16)],
        compiler_params=PARAMS,
        cost_estimate=pl.CostEstimate(
            flops=2 * rows * 4096 * 2 * HD, bytes_accessed=6 * 2**20, transcendentals=0
        ),
    )(place, *blocks, *parts, cosine, sine)


def project_q(place, blocks, own_wq, moved_wq, cosine, sine):
    rows = blocks[0].shape[0]
    return pl.pallas_call(
        functools.partial(project_q_kernel, rows),
        out_shape=jax.ShapeDtypeStruct((2 * rows, HD), jnp.bfloat16),
        in_specs=[SMEM] + [VMEM] * len(blocks) + [ANYWHERE] * 2 + [VMEM] * 2,
        out_specs=VMEM,
        scratch_shapes=[pltpu.VMEM(own_wq.shape, jnp.bfloat16), pltpu.SemaphoreType.DMA],
        compiler_params=PARAMS,
        cost_estimate=pl.CostEstimate(
            flops=2 * rows * 4096 * 2 * HD, bytes_accessed=6 * 2**20, transcendentals=0
        ),
    )(place, *blocks, own_wq, moved_wq, cosine, sine)


def attend_kernel(rows, steps, first, last, place, query, *refs):
    lines = refs[: len(steps)]
    refs = refs[len(steps) :]
    if not first:
        old_state, refs = refs[:3], refs[3:]
    if last:
        out, held, top, total, acc = refs
    else:
        top, total, acc, held = refs
    y, c, x = place[0], place[2], place[5]
    mine = y * NX + x

    def merge(keys, values, begin):
        scores = lax.dot_general(
            query[...], keys, (((1,), (1,)), ((), ())), preferred_element_type=jnp.float32
        )
        if begin:
            query_at = lax.rem(lax.broadcasted_iota(jnp.int32, scores.shape, 0), rows)
            key_at = lax.broadcasted_iota(jnp.int32, scores.shape, 1)
            scores = jnp.where(key_at <= query_at, scores, MASKED)
            peak = jnp.max(scores, axis=1, keepdims=True)
            peak = jnp.broadcast_to(peak, (2 * rows, HD))
        else:
            old = top[...]
            peak = jnp.maximum(old, jnp.max(scores, axis=1, keepdims=True))
        weights = jnp.exp2(scores - jnp.concatenate([peak] * (rows // HD), 1))
        sums = jnp.sum(weights, axis=1, keepdims=True)
        part = jnp.dot(weights.astype(jnp.bfloat16), values, preferred_element_type=jnp.float32)
        if begin:
            total[...] = jnp.broadcast_to(sums, (2 * rows, HD))
            acc[...] = part
        else:
            factor = jnp.exp2(old - peak)
            total[...] = total[...] * factor + sums
            acc[...] = acc[...] * factor + part
        top[...] = peak

    if not first:
        for new, old in zip((top, total, acc), old_state):
            new[...] = old[...]
    if first:
        merge(lines[0][0, :, :HD], lines[0][0, :, HD:], True)
    count = sum(line.shape[0] for line in lines)

    def step(block, carry):
        outer, inner, start = 0, 0, 0
        for line, (away, begin) in zip(lines, steps):
            here = (block >= start) & (block < start + line.shape[0])
            outer = jnp.where(here, away, outer)
            inner = jnp.where(here, lax.rem(4 + start - begin - block + 4, 4), inner)
            start += line.shape[0]
        dy = jnp.where(c == 0, outer, inner)
        dx = jnp.where(c == 0, inner, outer)
        theirs = lax.rem(y + dy, NY) * NX + lax.rem(x + dx, NX)

        @pl.when(theirs < mine)
        def _():
            start = 0
            for line in lines:

                @pl.when((block >= start) & (block < start + line.shape[0]))
                def _(line=line, start=start):
                    held[...] = line[block - start]

                start += line.shape[0]
            merge(held[:, :HD], held[:, HD:], False)

        return carry

    lax.fori_loop(1 if first else 0, count, step, 0)
    if last:
        context = acc[...] / total[...]
        out[...] = jnp.concatenate([context[:rows], context[rows:]], 1).astype(jnp.bfloat16)


def attend(place, query, lines, steps, state, last):
    rows = query.shape[0] // 2
    count = sum(line.shape[0] for line in lines)
    wide = (2 * rows, HD)
    scratch = [pltpu.VMEM((rows, 2 * HD), jnp.bfloat16)]
    if last:
        out_shape = jax.ShapeDtypeStruct((rows, 2 * HD), jnp.bfloat16)
        out_specs = VMEM
        scratch += [pltpu.VMEM(wide, jnp.float32)] * 3
    else:
        out_shape = (jax.ShapeDtypeStruct(wide, jnp.float32),) * 3
        out_specs = (VMEM,) * 3
    return pl.pallas_call(
        functools.partial(attend_kernel, rows, steps, not state, last),
        out_shape=out_shape,
        in_specs=[SMEM, VMEM] + [VMEM] * (len(lines) + len(state)),
        out_specs=out_specs,
        scratch_shapes=scratch,
        compiler_params=PARAMS,
        cost_estimate=pl.CostEstimate(
            flops=4 * 2 * rows * count * rows * HD,
            bytes_accessed=count * rows * 4 * HD,
            transcendentals=2 * rows * count * rows,
        ),
    )(place, query, *lines, *state)


def gather_inputs(tokens, query_weight, kv_weight, out_weight, place, c, z, same):
    def columns(core):
        part = lax.dynamic_slice_in_dim(kv_weight, (core * 4 + z // 2) * HD, HD, 2)
        return jnp.concatenate([part[0], part[1]], 1)

    mine, other = columns(c), columns(1 - c)
    own = [None] * NZ
    own[1] = send(tokens, swap_route(1))
    own[7] = send(tokens, swap_route(-1))
    own[0] = send_swapped(tokens, same)
    flipped = send(jnp.stack([mine, other]), FLIP_ROUTE)
    own[0], own[1], own[7], flipped, query_weight, out_weight = lax.optimization_barrier(
        (own[0], own[1], own[7], flipped, query_weight, out_weight)
    )
    others = send(jnp.stack([other, flipped[1]]), CORE_ROUTE)
    four = jnp.stack([mine, others[0], flipped[0], others[1]])
    first = send(four, y_chain(1))
    second = send(four, y_chain(-1))
    moved_wq = send(query_weight, SWAP)
    own[2] = send(own[1], z_chain(1))
    own[6] = send(own[7], z_chain(-1))
    own[3] = send(own[2], z_chain(1))
    own[5] = send(own[6], z_chain(-1))
    own[3], own[5], first, second = lax.optimization_barrier((own[3], own[5], first, second))
    far = send(first, y_chain(1))
    own[4] = send(own[3], z_chain(1))
    blocks = []
    for block in own:
        blocks += [block, send(block, CORE_ROUTE)]
    half_columns = out_weight.shape[1] // 2
    wo = lax.dynamic_slice_in_dim(out_weight, c * half_columns, half_columns, 1)
    near, last = order_columns(place, wo)
    moved_near = send(near, PAIR_ROUTE)
    far, moved_wq, last = lax.optimization_barrier((far, moved_wq, last))
    return blocks, [four, first, far, second], query_weight, moved_wq, near, moved_near, last


def scatter_sums(part_of, same):
    def add(part, arrived):
        return (part + arrived.astype(jnp.float32)).astype(jnp.bfloat16)

    long = send(part_of(4).astype(jnp.bfloat16), z_chain(1))
    short = send(part_of(5).astype(jnp.bfloat16), z_chain(-1))
    long = send(add(part_of(3), long), z_chain(1))
    short = send(add(part_of(6), short), z_chain(-1))
    middle = send_swapped(part_of(0).astype(jnp.bfloat16), same)
    long, short, middle = lax.optimization_barrier((long, short, middle))
    long = send(add(part_of(2), long), z_chain(1))
    short = send(add(part_of(7), short), swap_back_route(-1))
    long = send(add(part_of(1), long), swap_back_route(1))
    total = middle.astype(jnp.float32) + short.astype(jnp.float32) + long.astype(jnp.float32)
    return total.astype(jnp.bfloat16)


def shards(tokens, query_weight, kv_weight, out_weight):
    rows = tokens.shape[0]
    seq_rank = lax.axis_index("seq")
    tp_rank = lax.axis_index("tp")
    y, h, c = seq_rank // 4, (seq_rank // 2) % 2, seq_rank % 2
    l, z = tp_rank // NZ, tp_rank % NZ
    x = h * NL + l
    place = jnp.stack([y, h, c, l, z, x]).astype(jnp.int32)
    same = c == l

    blocks, wkv_parts, query_weight, moved_wq, near, moved_near, last = gather_inputs(
        tokens, query_weight, kv_weight, out_weight, place, c, z, same
    )

    positions = ((y * NX + x) * rows + jnp.arange(rows, dtype=jnp.int32)).astype(jnp.float32)
    frequency = ROTARY_BASE ** (-jnp.arange(HD // 2, dtype=jnp.float32) / (HD // 2))
    angles = positions[:, None] * frequency[None, :]
    cosine, sine = jnp.cos(angles), jnp.sin(angles)
    cosine = jnp.concatenate([cosine, cosine], 1)
    sine = jnp.concatenate([-sine, sine], 1)

    block = project_kv(place, blocks, wkv_parts, cosine, sine)
    line_first = send(block, line_route(1))
    line_second = send(block, line_route(-1))
    line_first, moved_near = lax.optimization_barrier((line_first, moved_near))
    line_far = send(line_first, line_route(1))
    query = project_q(place, blocks, query_weight, moved_wq, cosine, sine)
    line_far, line_second, query = lax.optimization_barrier((line_far, line_second, query))
    line = jnp.stack([block, line_first, line_far, line_second])
    first = send(line, cross_route(1))
    second = send(line, cross_route(-1))
    state = attend(place, query, [line], ((0, 0),), (), False)
    first, second, state = lax.optimization_barrier((first, second, state))
    far_low = send(first[:2], cross_route(1))
    far_high = send(second[2:], cross_route(-1))

    state = attend(place, query, [first, second], ((3, 0), (1, 0)), state, False)
    context = attend(place, query, [far_low, far_high], ((2, 0), (2, 2)), state, True)
    last, near, moved_near, context = lax.optimization_barrier((last, near, moved_near, context))
    near = jnp.concatenate([near, moved_near], 0)
    last = jnp.concatenate([last, send(last, PAIR_ROUTE)], 0)
    other = send(context, CORE_ROUTE)
    context = jnp.concatenate(
        [jnp.where(same, context, other), jnp.where(same, other, context)], 1
    )

    def part_of(steps):
        at = ORDER.index(steps)
        piece, at = (near, at * BLOCK) if at < 5 else (last, (at - 5) * BLOCK)
        return jnp.dot(context, piece[:, at : at + BLOCK], preferred_element_type=jnp.float32)

    return scatter_sums(part_of, same)


def solution(mesh):
    return jax.shard_map(
        shards,
        mesh=mesh,
        in_specs=(P("seq", "tp"), P(None, "tp"), P(None, "seq", None), P("tp", None)),
        out_specs=P("seq", "tp"),
        check_vma=False,
    )
```

```python
import functools

import jax
import jax.numpy as jnp
from jax import lax
from jax.experimental import pallas as pl
from jax.experimental.pallas import tpu as pltpu
from jax.sharding import PartitionSpec as P

HEADS = 32
KV_HEADS = 8
HD = 128
ROTARY_BASE = 500000.0
MASKED = -1e30
BOTH = ("seq", "tp")
NY, NH, NC, NL, NZ = 4, 2, 2, 2, 8
NX = NH * NL
BLOCK = 256
ARRIVAL = (0, 1, 7, 2, 6, 3, 5, 4)
ORDER = (4, 5, 3, 6, 0, 2, 7, 1)


def linear(y, h, c, l, z):
    return ((y * NH + h) * NC + c) * (NL * NZ) + l * NZ + z


def routes(move):
    pairs = []
    for y in range(NY):
        for h in range(NH):
            for c in range(NC):
                for l in range(NL):
                    for z in range(NZ):
                        pairs.append((linear(y, h, c, l, z), linear(*move(y, h, c, l, z))))
    return pairs


def sign_of(core):
    return 1 if core == 0 else -1


def swap_route(shift):
    return routes(lambda y, h, c, l, z: (y, h, l, c, (z + sign_of(l) * shift) % NZ))


def swap_back_route(shift):
    return routes(lambda y, h, c, l, z: (y, h, l, c, (z + sign_of(c) * shift) % NZ))


def z_chain(shift):
    return routes(lambda y, h, c, l, z: (y, h, c, l, (z + sign_of(c) * shift) % NZ))


def y_chain(shift):
    return routes(lambda y, h, c, l, z: ((y + sign_of(c) * shift) % NY, h, c, l, z))


def z_route(shift):
    return routes(lambda y, h, c, l, z: (y, h, c, l, (z + shift) % NZ))


def y_route(shift):
    return routes(lambda y, h, c, l, z: ((y + shift) % NY, h, c, l, z))


def x_route(shift):
    def move(y, h, c, l, z):
        x = (h * NL + l + shift) % NX
        return y, x // NL, c, x % NL, z

    return routes(move)


def line_route(shift):
    over_x, over_y = x_route(shift), y_route(shift)
    return routes_by_core(over_x, over_y)


def cross_route(shift):
    over_x, over_y = x_route(shift), y_route(shift)
    return routes_by_core(over_y, over_x)


def routes_by_core(first, second):
    pairs = []
    for one, other in zip(first, second):
        core = one[0] // (NL * NZ) % NC
        pairs.append(one if core == 0 else other)
    return pairs


CORE_ROUTE = routes(lambda y, h, c, l, z: (y, h, 1 - c, l, z))
PAIR_ROUTE = routes(lambda y, h, c, l, z: (y, h, c, 1 - l, z))
FLIP_ROUTE = routes(lambda y, h, c, l, z: (y, 1 - h, c, 1 - l, z))


def send(value, route):
    return lax.ppermute(value, BOTH, route)


SWAP = [(source, target) for source, target in swap_route(0) if source != target]


def send_swapped(value, same):
    return jnp.where(same, value, send(value, SWAP))


def rotated(vectors, cos, sin):
    half = HD // 2
    turned = jnp.concatenate([vectors[:, half:], vectors[:, :half]], 1)
    return vectors * cos + turned * sin


def project_rows(place, blocks, weight_of):
    c, z = place[2], place[4]
    acc = None
    for steps in ARRIVAL:
        for j in range(2):
            core = c if j == 0 else 1 - c
            feature = core * NZ + lax.rem(z + (2 * core - 1) * steps + NZ, NZ)
            part = jnp.dot(
                blocks[2 * steps + j][...],
                weight_of(feature),
                preferred_element_type=jnp.float32,
            )
            acc = part if acc is None else acc + part
    return acc


def project_kv_kernel(place, *refs):
    blocks, parts = refs[: 2 * NZ], refs[2 * NZ : 2 * NZ + 4]
    cosine, sine, out, wkv = refs[2 * NZ + 4 :]
    y, h, c = place[0], place[1], place[2]
    at = 0
    for part in parts:
        count = part.shape[0]
        wkv[at : at + count] = part[...]
        at += count

    def weight_of(feature):
        dy = lax.rem((2 * c - 1) * (feature // 4 - y) + NY, NY)
        dh = lax.rem(lax.rem(feature // 2, 2) + h, 2)
        dc = lax.rem(lax.rem(feature, 2) + c, 2)
        return wkv[(dy * 2 + dh) * 2 + dc]

    acc = project_rows(place, blocks, weight_of)
    out[:, :HD] = rotated(acc[:, :HD], cosine[...], sine[...]).astype(jnp.bfloat16)
    out[:, HD:] = acc[:, HD:].astype(jnp.bfloat16)


def project_q_kernel(rows, place, *refs):
    blocks = refs[: 2 * NZ]
    own_wq, moved_wq = refs[2 * NZ : 2 * NZ + 2]
    cosine, sine, out, wq, sem = refs[2 * NZ + 2 :]
    c, l = place[2], place[3]
    fetch_own = pltpu.make_async_copy(own_wq, wq, sem)
    fetch_moved = pltpu.make_async_copy(moved_wq, wq, sem)

    @pl.when(c == l)
    def _():
        fetch_own.start()

    @pl.when(c != l)
    def _():
        fetch_moved.start()

    fetch_own.wait()

    def weight_of(feature):
        return wq[pl.ds(pl.multiple_of(feature * BLOCK, BLOCK), BLOCK), :]

    acc = project_rows(place, blocks, weight_of)
    scale = HD**-0.5 * 1.4426950408889634
    for head in range(2):
        turned = rotated(acc[:, head * HD : (head + 1) * HD], cosine[...], sine[...])
        out[head * rows : (head + 1) * rows] = (turned * scale).astype(jnp.bfloat16)


VMEM = pl.BlockSpec(memory_space=pltpu.VMEM)
SMEM = pl.BlockSpec(memory_space=pltpu.SMEM)
ANYWHERE = pl.BlockSpec(memory_space=pl.ANY)
PARAMS = pltpu.CompilerParams(vmem_limit_bytes=48 * 2**20)


def order_kernel(place, weight, near, last):
    c, z = place[2], place[4]
    for at, steps in enumerate(ORDER):
        column = lax.rem(z + (1 - 2 * c) * steps + NZ, NZ)
        piece = weight[:, pl.ds(pl.multiple_of(column * BLOCK, BLOCK), BLOCK)]
        if at < 5:
            near[:, at * BLOCK : (at + 1) * BLOCK] = piece
        else:
            last[:, (at - 5) * BLOCK : (at - 4) * BLOCK] = piece


def order_columns(place, weight):
    rows = weight.shape[0]
    return pl.pallas_call(
        order_kernel,
        out_shape=(
            jax.ShapeDtypeStruct((rows, 5 * BLOCK), weight.dtype),
            jax.ShapeDtypeStruct((rows, 3 * BLOCK), weight.dtype),
        ),
        in_specs=[SMEM, VMEM],
        out_specs=(VMEM, VMEM),
        compiler_params=PARAMS,
        cost_estimate=pl.CostEstimate(flops=0, bytes_accessed=2 * 2**20, transcendentals=0),
    )(place, weight)


def project_kv(place, blocks, parts, cosine, sine):
    rows = blocks[0].shape[0]
    return pl.pallas_call(
        project_kv_kernel,
        out_shape=jax.ShapeDtypeStruct((rows, 2 * HD), jnp.bfloat16),
        in_specs=[SMEM] + [VMEM] * (len(blocks) + len(parts) + 2),
        out_specs=VMEM,
        scratch_shapes=[pltpu.VMEM((16, BLOCK, 2 * HD), jnp.bfloat16)],
        compiler_params=PARAMS,
        cost_estimate=pl.CostEstimate(
            flops=2 * rows * 4096 * 2 * HD, bytes_accessed=6 * 2**20, transcendentals=0
        ),
    )(place, *blocks, *parts, cosine, sine)


def project_q(place, blocks, own_wq, moved_wq, cosine, sine):
    rows = blocks[0].shape[0]
    return pl.pallas_call(
        functools.partial(project_q_kernel, rows),
        out_shape=jax.ShapeDtypeStruct((2 * rows, HD), jnp.bfloat16),
        in_specs=[SMEM] + [VMEM] * len(blocks) + [ANYWHERE] * 2 + [VMEM] * 2,
        out_specs=VMEM,
        scratch_shapes=[pltpu.VMEM(own_wq.shape, jnp.bfloat16), pltpu.SemaphoreType.DMA],
        compiler_params=PARAMS,
        cost_estimate=pl.CostEstimate(
            flops=2 * rows * 4096 * 2 * HD, bytes_accessed=6 * 2**20, transcendentals=0
        ),
    )(place, *blocks, own_wq, moved_wq, cosine, sine)


def attend_kernel(rows, steps, first, last, place, query, *refs):
    lines = refs[: len(steps)]
    refs = refs[len(steps) :]
    if not first:
        old_state, refs = refs[:3], refs[3:]
    if last:
        out, held, top, total, acc = refs
    else:
        top, total, acc, held = refs
    y, c, x = place[0], place[2], place[5]
    mine = y * NX + x

    def merge(keys, values, begin):
        scores = lax.dot_general(
            query[...], keys, (((1,), (1,)), ((), ())), preferred_element_type=jnp.float32
        )
        if begin:
            query_at = lax.rem(lax.broadcasted_iota(jnp.int32, scores.shape, 0), rows)
            key_at = lax.broadcasted_iota(jnp.int32, scores.shape, 1)
            scores = jnp.where(key_at <= query_at, scores, MASKED)
            peak = jnp.max(scores, axis=1, keepdims=True)
            peak = jnp.broadcast_to(peak, (2 * rows, HD))
        else:
            old = top[...]
            peak = jnp.maximum(old, jnp.max(scores, axis=1, keepdims=True))
        weights = jnp.exp2(scores - jnp.concatenate([peak] * (rows // HD), 1))
        sums = jnp.sum(weights, axis=1, keepdims=True)
        part = jnp.dot(weights.astype(jnp.bfloat16), values, preferred_element_type=jnp.float32)
        if begin:
            total[...] = jnp.broadcast_to(sums, (2 * rows, HD))
            acc[...] = part
        else:
            factor = jnp.exp2(old - peak)
            total[...] = total[...] * factor + sums
            acc[...] = acc[...] * factor + part
        top[...] = peak

    if not first:
        for new, old in zip((top, total, acc), old_state):
            new[...] = old[...]
    if first:
        merge(lines[0][0, :, :HD], lines[0][0, :, HD:], True)
    count = sum(line.shape[0] for line in lines)

    def step(block, carry):
        outer, inner, start = 0, 0, 0
        for line, (away, begin) in zip(lines, steps):
            here = (block >= start) & (block < start + line.shape[0])
            outer = jnp.where(here, away, outer)
            inner = jnp.where(here, lax.rem(4 + start - begin - block + 4, 4), inner)
            start += line.shape[0]
        dy = jnp.where(c == 0, outer, inner)
        dx = jnp.where(c == 0, inner, outer)
        theirs = lax.rem(y + dy, NY) * NX + lax.rem(x + dx, NX)

        @pl.when(theirs < mine)
        def _():
            start = 0
            for line in lines:

                @pl.when((block >= start) & (block < start + line.shape[0]))
                def _(line=line, start=start):
                    held[...] = line[block - start]

                start += line.shape[0]
            merge(held[:, :HD], held[:, HD:], False)

        return carry

    lax.fori_loop(1 if first else 0, count, step, 0)
    if last:
        context = acc[...] / total[...]
        out[...] = jnp.concatenate([context[:rows], context[rows:]], 1).astype(jnp.bfloat16)


def attend(place, query, lines, steps, state, last):
    rows = query.shape[0] // 2
    count = sum(line.shape[0] for line in lines)
    wide = (2 * rows, HD)
    scratch = [pltpu.VMEM((rows, 2 * HD), jnp.bfloat16)]
    if last:
        out_shape = jax.ShapeDtypeStruct((rows, 2 * HD), jnp.bfloat16)
        out_specs = VMEM
        scratch += [pltpu.VMEM(wide, jnp.float32)] * 3
    else:
        out_shape = (jax.ShapeDtypeStruct(wide, jnp.float32),) * 3
        out_specs = (VMEM,) * 3
    return pl.pallas_call(
        functools.partial(attend_kernel, rows, steps, not state, last),
        out_shape=out_shape,
        in_specs=[SMEM, VMEM] + [VMEM] * (len(lines) + len(state)),
        out_specs=out_specs,
        scratch_shapes=scratch,
        compiler_params=PARAMS,
        cost_estimate=pl.CostEstimate(
            flops=4 * 2 * rows * count * rows * HD,
            bytes_accessed=count * rows * 4 * HD,
            transcendentals=2 * rows * count * rows,
        ),
    )(place, query, *lines, *state)


def gather_inputs(tokens, query_weight, kv_weight, out_weight, place, c, z, same):
    def columns(core):
        part = lax.dynamic_slice_in_dim(kv_weight, (core * 4 + z // 2) * HD, HD, 2)
        return jnp.concatenate([part[0], part[1]], 1)

    mine, other = columns(c), columns(1 - c)
    own = [None] * NZ
    own[1] = send(tokens, swap_route(1))
    own[7] = send(tokens, swap_route(-1))
    own[0] = send_swapped(tokens, same)
    flipped = send(jnp.stack([mine, other]), FLIP_ROUTE)
    own[0], own[1], own[7], flipped, query_weight, out_weight = lax.optimization_barrier(
        (own[0], own[1], own[7], flipped, query_weight, out_weight)
    )
    others = send(jnp.stack([other, flipped[1]]), CORE_ROUTE)
    four = jnp.stack([mine, others[0], flipped[0], others[1]])
    first = send(four, y_chain(1))
    second = send(four, y_chain(-1))
    moved_wq = send(query_weight, SWAP)
    own[2] = send(own[1], z_chain(1))
    own[6] = send(own[7], z_chain(-1))
    own[3] = send(own[2], z_chain(1))
    own[5] = send(own[6], z_chain(-1))
    own[4] = send(own[3], z_chain(1))
    own[3], own[5], first, second = lax.optimization_barrier((own[3], own[5], first, second))
    far = send(first, y_chain(1))
    blocks = []
    for block in own:
        blocks += [block, send(block, CORE_ROUTE)]
    half_columns = out_weight.shape[1] // 2
    wo = lax.dynamic_slice_in_dim(out_weight, c * half_columns, half_columns, 1)
    near, last = order_columns(place, wo)
    moved_near = send(near, PAIR_ROUTE)
    far, moved_wq, last = lax.optimization_barrier((far, moved_wq, last))
    return blocks, [four, first, far, second], query_weight, moved_wq, near, moved_near, last


def scatter_sums(part_of, same):
    def add(part, arrived):
        return (part + arrived.astype(jnp.float32)).astype(jnp.bfloat16)

    long = send(part_of(4).astype(jnp.bfloat16), z_chain(1))
    short = send(part_of(5).astype(jnp.bfloat16), z_chain(-1))
    long = send(add(part_of(3), long), z_chain(1))
    short = send(add(part_of(6), short), z_chain(-1))
    middle = send_swapped(part_of(0).astype(jnp.bfloat16), same)
    long, short, middle = lax.optimization_barrier((long, short, middle))
    long = send(add(part_of(2), long), z_chain(1))
    short = send(add(part_of(7), short), swap_back_route(-1))
    long = send(add(part_of(1), long), swap_back_route(1))
    total = middle.astype(jnp.float32) + short.astype(jnp.float32) + long.astype(jnp.float32)
    return total.astype(jnp.bfloat16)


def shards(tokens, query_weight, kv_weight, out_weight):
    rows = tokens.shape[0]
    seq_rank = lax.axis_index("seq")
    tp_rank = lax.axis_index("tp")
    y, h, c = seq_rank // 4, (seq_rank // 2) % 2, seq_rank % 2
    l, z = tp_rank // NZ, tp_rank % NZ
    x = h * NL + l
    place = jnp.stack([y, h, c, l, z, x]).astype(jnp.int32)
    same = c == l

    blocks, wkv_parts, query_weight, moved_wq, near, moved_near, last = gather_inputs(
        tokens, query_weight, kv_weight, out_weight, place, c, z, same
    )

    positions = ((y * NX + x) * rows + jnp.arange(rows, dtype=jnp.int32)).astype(jnp.float32)
    frequency = ROTARY_BASE ** (-jnp.arange(HD // 2, dtype=jnp.float32) / (HD // 2))
    angles = positions[:, None] * frequency[None, :]
    cosine, sine = jnp.cos(angles), jnp.sin(angles)
    cosine = jnp.concatenate([cosine, cosine], 1)
    sine = jnp.concatenate([-sine, sine], 1)

    block = project_kv(place, blocks, wkv_parts, cosine, sine)
    line_first = send(block, line_route(1))
    line_second = send(block, line_route(-1))
    line_first, moved_near = lax.optimization_barrier((line_first, moved_near))
    line_far = send(line_first, line_route(1))
    query = project_q(place, blocks, query_weight, moved_wq, cosine, sine)
    line_far, line_second, query = lax.optimization_barrier((line_far, line_second, query))
    line = jnp.stack([block, line_first, line_far, line_second])
    first = send(line, cross_route(1))
    second = send(line, cross_route(-1))
    state = attend(place, query, [line], ((0, 0),), (), False)
    first, second, state = lax.optimization_barrier((first, second, state))
    far_low = send(first[:2], cross_route(1))
    far_high = send(second[2:], cross_route(-1))

    state = attend(place, query, [first, second], ((3, 0), (1, 0)), state, False)
    context = attend(place, query, [far_low, far_high], ((2, 0), (2, 2)), state, True)
    last, near, moved_near, context = lax.optimization_barrier((last, near, moved_near, context))
    near = jnp.concatenate([near, moved_near], 0)
    last = jnp.concatenate([last, send(last, PAIR_ROUTE)], 0)
    other = send(context, CORE_ROUTE)
    context = jnp.concatenate(
        [jnp.where(same, context, other), jnp.where(same, other, context)], 1
    )

    def part_of(steps):
        at = ORDER.index(steps)
        piece, at = (near, at * BLOCK) if at < 5 else (last, (at - 5) * BLOCK)
        return jnp.dot(context, piece[:, at : at + BLOCK], preferred_element_type=jnp.float32)

    return scatter_sums(part_of, same)


def solution(mesh):
    return jax.shard_map(
        shards,
        mesh=mesh,
        in_specs=(P("seq", "tp"), P(None, "tp"), P(None, "seq", None), P("tp", None)),
        out_specs=P("seq", "tp"),
        check_vma=False,
    )
```

```python
import functools

import jax
import jax.numpy as jnp
from jax import lax
from jax.experimental import pallas as pl
from jax.experimental.pallas import tpu as pltpu
from jax.sharding import PartitionSpec as P

HEADS = 32
KV_HEADS = 8
HD = 128
ROTARY_BASE = 500000.0
MASKED = -1e30
BOTH = ("seq", "tp")
NY, NH, NC, NL, NZ = 4, 2, 2, 2, 8
NX = NH * NL
BLOCK = 256
ARRIVAL = (0, 1, 7, 2, 6, 3, 5, 4)
ORDER = (4, 5, 3, 6, 0, 2, 7, 1)


def linear(y, h, c, l, z):
    return ((y * NH + h) * NC + c) * (NL * NZ) + l * NZ + z


def routes(move):
    pairs = []
    for y in range(NY):
        for h in range(NH):
            for c in range(NC):
                for l in range(NL):
                    for z in range(NZ):
                        pairs.append((linear(y, h, c, l, z), linear(*move(y, h, c, l, z))))
    return pairs


def sign_of(core):
    return 1 if core == 0 else -1


def swap_route(shift):
    return routes(lambda y, h, c, l, z: (y, h, l, c, (z + sign_of(l) * shift) % NZ))


def swap_back_route(shift):
    return routes(lambda y, h, c, l, z: (y, h, l, c, (z + sign_of(c) * shift) % NZ))


def z_chain(shift):
    return routes(lambda y, h, c, l, z: (y, h, c, l, (z + sign_of(c) * shift) % NZ))


def y_chain(shift):
    return routes(lambda y, h, c, l, z: ((y + sign_of(c) * shift) % NY, h, c, l, z))


def z_route(shift):
    return routes(lambda y, h, c, l, z: (y, h, c, l, (z + shift) % NZ))


def y_route(shift):
    return routes(lambda y, h, c, l, z: ((y + shift) % NY, h, c, l, z))


def x_route(shift):
    def move(y, h, c, l, z):
        x = (h * NL + l + shift) % NX
        return y, x // NL, c, x % NL, z

    return routes(move)


def line_route(shift):
    over_x, over_y = x_route(shift), y_route(shift)
    return routes_by_core(over_x, over_y)


def cross_route(shift):
    over_x, over_y = x_route(shift), y_route(shift)
    return routes_by_core(over_y, over_x)


def routes_by_core(first, second):
    pairs = []
    for one, other in zip(first, second):
        core = one[0] // (NL * NZ) % NC
        pairs.append(one if core == 0 else other)
    return pairs


CORE_ROUTE = routes(lambda y, h, c, l, z: (y, h, 1 - c, l, z))
PAIR_ROUTE = routes(lambda y, h, c, l, z: (y, h, c, 1 - l, z))
FLIP_ROUTE = routes(lambda y, h, c, l, z: (y, 1 - h, c, 1 - l, z))


def send(value, route):
    return lax.ppermute(value, BOTH, route)


SWAP = [(source, target) for source, target in swap_route(0) if source != target]


def send_swapped(value, same):
    return jnp.where(same, value, send(value, SWAP))


def rotated(vectors, cos, sin):
    half = HD // 2
    turned = jnp.concatenate([vectors[:, half:], vectors[:, :half]], 1)
    return vectors * cos + turned * sin


def project_rows(place, blocks, weight_of):
    c, z = place[2], place[4]
    acc = None
    for steps in ARRIVAL:
        for j in range(2):
            core = c if j == 0 else 1 - c
            feature = core * NZ + lax.rem(z + (2 * core - 1) * steps + NZ, NZ)
            part = jnp.dot(
                blocks[2 * steps + j][...],
                weight_of(feature),
                preferred_element_type=jnp.float32,
            )
            acc = part if acc is None else acc + part
    return acc


def project_kv_kernel(place, *refs):
    blocks, parts = refs[: 2 * NZ], refs[2 * NZ : 2 * NZ + 4]
    cosine, sine, out, wkv = refs[2 * NZ + 4 :]
    y, h, c = place[0], place[1], place[2]
    at = 0
    for part in parts:
        count = part.shape[0]
        wkv[at : at + count] = part[...]
        at += count

    def weight_of(feature):
        dy = lax.rem((2 * c - 1) * (feature // 4 - y) + NY, NY)
        dh = lax.rem(lax.rem(feature // 2, 2) + h, 2)
        dc = lax.rem(lax.rem(feature, 2) + c, 2)
        return wkv[(dy * 2 + dh) * 2 + dc]

    acc = project_rows(place, blocks, weight_of)
    out[:, :HD] = rotated(acc[:, :HD], cosine[...], sine[...]).astype(jnp.bfloat16)
    out[:, HD:] = acc[:, HD:].astype(jnp.bfloat16)


def project_q_kernel(rows, place, *refs):
    blocks = refs[: 2 * NZ]
    own_wq, moved_wq = refs[2 * NZ : 2 * NZ + 2]
    cosine, sine, out, wq, sem = refs[2 * NZ + 2 :]
    c, l = place[2], place[3]
    fetch_own = pltpu.make_async_copy(own_wq, wq, sem)
    fetch_moved = pltpu.make_async_copy(moved_wq, wq, sem)

    @pl.when(c == l)
    def _():
        fetch_own.start()

    @pl.when(c != l)
    def _():
        fetch_moved.start()

    fetch_own.wait()

    def weight_of(feature):
        return wq[pl.ds(pl.multiple_of(feature * BLOCK, BLOCK), BLOCK), :]

    acc = project_rows(place, blocks, weight_of)
    scale = HD**-0.5 * 1.4426950408889634
    for head in range(2):
        turned = rotated(acc[:, head * HD : (head + 1) * HD], cosine[...], sine[...])
        out[head * rows : (head + 1) * rows] = (turned * scale).astype(jnp.bfloat16)


VMEM = pl.BlockSpec(memory_space=pltpu.VMEM)
SMEM = pl.BlockSpec(memory_space=pltpu.SMEM)
ANYWHERE = pl.BlockSpec(memory_space=pl.ANY)
PARAMS = pltpu.CompilerParams(vmem_limit_bytes=48 * 2**20)


def order_kernel(place, weight, near, last):
    c, z = place[2], place[4]
    for at, steps in enumerate(ORDER):
        column = lax.rem(z + (1 - 2 * c) * steps + NZ, NZ)
        piece = weight[:, pl.ds(pl.multiple_of(column * BLOCK, BLOCK), BLOCK)]
        if at < 5:
            near[:, at * BLOCK : (at + 1) * BLOCK] = piece
        else:
            last[:, (at - 5) * BLOCK : (at - 4) * BLOCK] = piece


def order_columns(place, weight):
    rows = weight.shape[0]
    return pl.pallas_call(
        order_kernel,
        out_shape=(
            jax.ShapeDtypeStruct((rows, 5 * BLOCK), weight.dtype),
            jax.ShapeDtypeStruct((rows, 3 * BLOCK), weight.dtype),
        ),
        in_specs=[SMEM, VMEM],
        out_specs=(VMEM, VMEM),
        compiler_params=PARAMS,
        cost_estimate=pl.CostEstimate(flops=0, bytes_accessed=2 * 2**20, transcendentals=0),
    )(place, weight)


def project_kv(place, blocks, parts, cosine, sine):
    rows = blocks[0].shape[0]
    return pl.pallas_call(
        project_kv_kernel,
        out_shape=jax.ShapeDtypeStruct((rows, 2 * HD), jnp.bfloat16),
        in_specs=[SMEM] + [VMEM] * (len(blocks) + len(parts) + 2),
        out_specs=VMEM,
        scratch_shapes=[pltpu.VMEM((16, BLOCK, 2 * HD), jnp.bfloat16)],
        compiler_params=PARAMS,
        cost_estimate=pl.CostEstimate(
            flops=2 * rows * 4096 * 2 * HD, bytes_accessed=6 * 2**20, transcendentals=0
        ),
    )(place, *blocks, *parts, cosine, sine)


def project_q(place, blocks, own_wq, moved_wq, cosine, sine):
    rows = blocks[0].shape[0]
    return pl.pallas_call(
        functools.partial(project_q_kernel, rows),
        out_shape=jax.ShapeDtypeStruct((2 * rows, HD), jnp.bfloat16),
        in_specs=[SMEM] + [VMEM] * len(blocks) + [ANYWHERE] * 2 + [VMEM] * 2,
        out_specs=VMEM,
        scratch_shapes=[pltpu.VMEM(own_wq.shape, jnp.bfloat16), pltpu.SemaphoreType.DMA],
        compiler_params=PARAMS,
        cost_estimate=pl.CostEstimate(
            flops=2 * rows * 4096 * 2 * HD, bytes_accessed=6 * 2**20, transcendentals=0
        ),
    )(place, *blocks, own_wq, moved_wq, cosine, sine)


def attend_kernel(rows, steps, first, last, place, query, *refs):
    lines = refs[: len(steps)]
    refs = refs[len(steps) :]
    if not first:
        old_state, refs = refs[:3], refs[3:]
    if last:
        out, held, top, total, acc = refs
    else:
        top, total, acc, held = refs
    y, c, x = place[0], place[2], place[5]
    mine = y * NX + x

    def merge(keys, values, begin):
        scores = lax.dot_general(
            query[...], keys, (((1,), (1,)), ((), ())), preferred_element_type=jnp.float32
        )
        if begin:
            query_at = lax.rem(lax.broadcasted_iota(jnp.int32, scores.shape, 0), rows)
            key_at = lax.broadcasted_iota(jnp.int32, scores.shape, 1)
            scores = jnp.where(key_at <= query_at, scores, MASKED)
            peak = jnp.max(scores, axis=1, keepdims=True)
            peak = jnp.broadcast_to(peak, (2 * rows, HD))
        else:
            old = top[...]
            peak = jnp.maximum(old, jnp.max(scores, axis=1, keepdims=True))
        weights = jnp.exp2(scores - jnp.concatenate([peak] * (rows // HD), 1))
        sums = jnp.sum(weights, axis=1, keepdims=True)
        part = jnp.dot(weights.astype(jnp.bfloat16), values, preferred_element_type=jnp.float32)
        if begin:
            total[...] = jnp.broadcast_to(sums, (2 * rows, HD))
            acc[...] = part
        else:
            factor = jnp.exp2(old - peak)
            total[...] = total[...] * factor + sums
            acc[...] = acc[...] * factor + part
        top[...] = peak

    if not first:
        for new, old in zip((top, total, acc), old_state):
            new[...] = old[...]
    if first:
        merge(lines[0][0, :, :HD], lines[0][0, :, HD:], True)
    count = sum(line.shape[0] for line in lines)

    def step(block, carry):
        outer, inner, start = 0, 0, 0
        for line, (away, begin) in zip(lines, steps):
            here = (block >= start) & (block < start + line.shape[0])
            outer = jnp.where(here, away, outer)
            inner = jnp.where(here, lax.rem(4 + start - begin - block + 4, 4), inner)
            start += line.shape[0]
        dy = jnp.where(c == 0, outer, inner)
        dx = jnp.where(c == 0, inner, outer)
        theirs = lax.rem(y + dy, NY) * NX + lax.rem(x + dx, NX)

        @pl.when(theirs < mine)
        def _():
            start = 0
            for line in lines:

                @pl.when((block >= start) & (block < start + line.shape[0]))
                def _(line=line, start=start):
                    held[...] = line[block - start]

                start += line.shape[0]
            merge(held[:, :HD], held[:, HD:], False)

        return carry

    lax.fori_loop(1 if first else 0, count, step, 0)
    if last:
        context = acc[...] / total[...]
        out[...] = jnp.concatenate([context[:rows], context[rows:]], 1).astype(jnp.bfloat16)


def attend(place, query, lines, steps, state, last):
    rows = query.shape[0] // 2
    count = sum(line.shape[0] for line in lines)
    wide = (2 * rows, HD)
    scratch = [pltpu.VMEM((rows, 2 * HD), jnp.bfloat16)]
    if last:
        out_shape = jax.ShapeDtypeStruct((rows, 2 * HD), jnp.bfloat16)
        out_specs = VMEM
        scratch += [pltpu.VMEM(wide, jnp.float32)] * 3
    else:
        out_shape = (jax.ShapeDtypeStruct(wide, jnp.float32),) * 3
        out_specs = (VMEM,) * 3
    return pl.pallas_call(
        functools.partial(attend_kernel, rows, steps, not state, last),
        out_shape=out_shape,
        in_specs=[SMEM, VMEM] + [VMEM] * (len(lines) + len(state)),
        out_specs=out_specs,
        scratch_shapes=scratch,
        compiler_params=PARAMS,
        cost_estimate=pl.CostEstimate(
            flops=4 * 2 * rows * count * rows * HD,
            bytes_accessed=count * rows * 4 * HD,
            transcendentals=2 * rows * count * rows,
        ),
    )(place, query, *lines, *state)


def gather_inputs(tokens, query_weight, kv_weight, out_weight, place, c, z, same):
    def columns(core):
        part = lax.dynamic_slice_in_dim(kv_weight, (core * 4 + z // 2) * HD, HD, 2)
        return jnp.concatenate([part[0], part[1]], 1)

    mine, other = columns(c), columns(1 - c)
    own = [None] * NZ
    own[1] = send(tokens, swap_route(1))
    own[7] = send(tokens, swap_route(-1))
    own[0] = send_swapped(tokens, same)
    flipped = send(jnp.stack([mine, other]), FLIP_ROUTE)
    own[0], own[1], own[7], flipped, query_weight, out_weight = lax.optimization_barrier(
        (own[0], own[1], own[7], flipped, query_weight, out_weight)
    )
    others = send(jnp.stack([other, flipped[1]]), CORE_ROUTE)
    four = jnp.stack([mine, others[0], flipped[0], others[1]])
    first = send(four, y_chain(1))
    second = send(four, y_chain(-1))
    moved_wq = send(query_weight, SWAP)
    own[2] = send(own[1], z_chain(1))
    own[6] = send(own[7], z_chain(-1))
    own[3] = send(own[2], z_chain(1))
    own[5] = send(own[6], z_chain(-1))
    own[3], own[5], first, second = lax.optimization_barrier((own[3], own[5], first, second))
    far = send(first, y_chain(1))
    own[4] = send(own[3], z_chain(1))
    blocks = []
    for block in own:
        blocks += [block, send(block, CORE_ROUTE)]
    half_columns = out_weight.shape[1] // 2
    wo = lax.dynamic_slice_in_dim(out_weight, c * half_columns, half_columns, 1)
    near, last = order_columns(place, wo)
    moved_near = send(near, PAIR_ROUTE)
    far, moved_wq, last = lax.optimization_barrier((far, moved_wq, last))
    return blocks, [four, first, far, second], query_weight, moved_wq, near, moved_near, last


def scatter_sums(part_of, same):
    def add(part, arrived):
        return (part + arrived.astype(jnp.float32)).astype(jnp.bfloat16)

    long = send(part_of(4).astype(jnp.bfloat16), z_chain(1))
    short = send(part_of(5).astype(jnp.bfloat16), z_chain(-1))
    long = send(add(part_of(3), long), z_chain(1))
    short = send(add(part_of(6), short), z_chain(-1))
    middle = send_swapped(part_of(0).astype(jnp.bfloat16), same)
    long = send(add(part_of(2), long), z_chain(1))
    short = send(add(part_of(7), short), swap_back_route(-1))
    long, middle = lax.optimization_barrier((long, middle))
    long = send(add(part_of(1), long), swap_back_route(1))
    total = middle.astype(jnp.float32) + short.astype(jnp.float32) + long.astype(jnp.float32)
    return total.astype(jnp.bfloat16)


def shards(tokens, query_weight, kv_weight, out_weight):
    rows = tokens.shape[0]
    seq_rank = lax.axis_index("seq")
    tp_rank = lax.axis_index("tp")
    y, h, c = seq_rank // 4, (seq_rank // 2) % 2, seq_rank % 2
    l, z = tp_rank // NZ, tp_rank % NZ
    x = h * NL + l
    place = jnp.stack([y, h, c, l, z, x]).astype(jnp.int32)
    same = c == l

    blocks, wkv_parts, query_weight, moved_wq, near, moved_near, last = gather_inputs(
        tokens, query_weight, kv_weight, out_weight, place, c, z, same
    )

    positions = ((y * NX + x) * rows + jnp.arange(rows, dtype=jnp.int32)).astype(jnp.float32)
    frequency = ROTARY_BASE ** (-jnp.arange(HD // 2, dtype=jnp.float32) / (HD // 2))
    angles = positions[:, None] * frequency[None, :]
    cosine, sine = jnp.cos(angles), jnp.sin(angles)
    cosine = jnp.concatenate([cosine, cosine], 1)
    sine = jnp.concatenate([-sine, sine], 1)

    block = project_kv(place, blocks, wkv_parts, cosine, sine)
    line_first = send(block, line_route(1))
    line_second = send(block, line_route(-1))
    line_first, moved_near = lax.optimization_barrier((line_first, moved_near))
    line_far = send(line_first, line_route(1))
    query = project_q(place, blocks, query_weight, moved_wq, cosine, sine)
    line_far, line_second, query = lax.optimization_barrier((line_far, line_second, query))
    line = jnp.stack([block, line_first, line_far, line_second])
    first = send(line, cross_route(1))
    second = send(line, cross_route(-1))
    state = attend(place, query, [line], ((0, 0),), (), False)
    first, second, state = lax.optimization_barrier((first, second, state))
    far_low = send(first[:2], cross_route(1))
    far_high = send(second[2:], cross_route(-1))

    state = attend(place, query, [first, second], ((3, 0), (1, 0)), state, False)
    context = attend(place, query, [far_low, far_high], ((2, 0), (2, 2)), state, True)
    last, near, moved_near, context = lax.optimization_barrier((last, near, moved_near, context))
    near = jnp.concatenate([near, moved_near], 0)
    last = jnp.concatenate([last, send(last, PAIR_ROUTE)], 0)
    other = send(context, CORE_ROUTE)
    context = jnp.concatenate(
        [jnp.where(same, context, other), jnp.where(same, other, context)], 1
    )

    def part_of(steps):
        at = ORDER.index(steps)
        piece, at = (near, at * BLOCK) if at < 5 else (last, (at - 5) * BLOCK)
        return jnp.dot(context, piece[:, at : at + BLOCK], preferred_element_type=jnp.float32)

    return scatter_sums(part_of, same)


def solution(mesh):
    return jax.shard_map(
        shards,
        mesh=mesh,
        in_specs=(P("seq", "tp"), P(None, "tp"), P(None, "seq", None), P("tp", None)),
        out_specs=P("seq", "tp"),
        check_vma=False,
    )
```
